512 devices in a mesh: cuts: 64 (over x, z_lo, y), circ: 8 (over z_hi, core).
Axes of the slice: x: 4, y: 8, z: 8 (z_hi: 4, z_lo: 2; z = z_hi * 2 + z_lo), core: 2. Of those that a mesh axis runs over, the one named last changes fastest.
Arguments:
- sources: bfloat16 [64, 8, 8, 16, 1024], P('cuts', None, 'circ'), may hold values from -6 to 6
- block_inverse: bfloat16 [8, 1024, 1024], P('circ'), may hold values from -0.0115625 to 0.92
- memory_factor: float32 [64, 8, 1024], P('cuts', 'circ'), may hold values from 0.5 to 1
- coupling_target: int32 [8, 4], P('circ'), may hold values from 0 to 7, as said below
- coupling_weight: bfloat16 [8, 4, 128, 1024], P('circ'), may hold values from -0.09375 to 0.09375
- coarse_decay: float32 [64, 8, 1024], P('cuts', 'circ'), may hold values from 0.2 to 0.995
- initial_state: float32 [8, 16, 1024], P('circ'), may hold values from -6 to 6
Outputs:
- slice_starts: float32 [64, 8, 16, 1024], P('cuts', 'circ')
- waveform: bfloat16 [64, 8, 8, 16, 1024], P('cuts', None, 'circ')
The draws below stay inside these ranges and needn't reach their ends.
Inputs may be any that keep to these rules, and one draw needn't show every extreme that they name: `coupling_target`: row j names 4 subcircuits, j itself among them possibly; a row may name one subcircuit twice.
All inputs are finite; a program needn't handle non-finite values.
Results may differ from the reference program's by a relative error of at most 0.007.
Values sent between devices are 32-bit elements; how exact they have to be, the bound alone decides.
No kernel may reach another device: no remote copies, remote signals or barrier semaphores. Data moves between devices by JAX's collectives and lax.ppermute only.
A program may use at most 64 MiB of HBM per device.

```python
import math
import jax
import jax.numpy as jnp
from jax import lax

CIRCUIT_NODES = 1024
PORTS = 128
SCEN = 16
STEPS = 8
SWEEPS = 3
ITERS = 2
KC = 4
SUB_DEV = 1
SUBCIRCUIT_COUNT = 8
TIME_SLICES = 64
N_CIRC = 8


def draw_block_inverse(key, part):
    key_diag = jax.random.fold_in(key, 11)
    key_off = jax.random.fold_in(key, 12)
    spread = 0.12 * CIRCUIT_NODES ** (-0.5)
    diagonal = jnp.exp(jax.random.uniform(key_diag, (SUBCIRCUIT_COUNT, CIRCUIT_NODES), jnp.float32, jnp.log(0.3), jnp.log(0.85)))
    offdiag = jnp.clip(jax.random.normal(key_off, (SUBCIRCUIT_COUNT, CIRCUIT_NODES, CIRCUIT_NODES), jnp.float32), -3.0, 3.0) * spread
    identity = jnp.eye(CIRCUIT_NODES, dtype=jnp.float32)
    return (offdiag + diagonal[:, :, None] * identity[None]).astype(jnp.bfloat16)


def draw_coupling_target(key, part):
    targets = jax.random.randint(jax.random.fold_in(key, 21), (SUBCIRCUIT_COUNT, KC), 0, SUBCIRCUIT_COUNT)
    return targets.astype(jnp.int32)


def draw_coarse_decay(key, part):
    random_key_list = [jax.random.fold_in(key, 31 + offset) for offset in range(5)]
    slow_share = 0.5
    slow_mask = jax.random.uniform(random_key_list[0], (SUBCIRCUIT_COUNT, CIRCUIT_NODES), jnp.float32) < slow_share
    sluggish_rate = jax.random.uniform(random_key_list[1], (TIME_SLICES, SUBCIRCUIT_COUNT, CIRCUIT_NODES), jnp.float32, 0.97, 0.995)
    fast_rate = jax.random.uniform(random_key_list[2], (TIME_SLICES, SUBCIRCUIT_COUNT, CIRCUIT_NODES), jnp.float32, 0.2, 0.6)
    spike_slices = jax.random.randint(random_key_list[3], (3,), 0, TIME_SLICES)
    spike_active = jnp.any(jnp.arange(TIME_SLICES)[:, None] == spike_slices[None, :], axis=1)
    spike_multiplier = jax.random.uniform(random_key_list[4], (TIME_SLICES, SUBCIRCUIT_COUNT, CIRCUIT_NODES), jnp.float32, 0.5, 0.8)
    sluggish_rate = jnp.where(spike_active[:, None, None], sluggish_rate * spike_multiplier, sluggish_rate)
    return jnp.where(slow_mask[None], sluggish_rate, fast_rate).astype(jnp.float32)


def level_of(key, dims, cuts, low, largest):
    def one(position, blocks):
        steps = jax.random.uniform(jax.random.fold_in(jax.random.fold_in(key, 6), position), (blocks,), jnp.float32, low / len(cuts), largest / len(cuts))
        return jnp.repeat(jnp.exp(steps), dims[position] // blocks).reshape((-1,) + (1,) * (len(dims) - position - 1))

    loudness = one(*cuts[0])
    for cut in cuts[1:]:
        loudness = loudness * one(*cut)
    return loudness


def normal_values(own_key, extent, deviation, most, pieces=(), held_as=jnp.bfloat16):
    array = jax.random.normal(own_key, extent, jnp.float32) * deviation
    if len(pieces) > 0:
        array = level_of(own_key, extent, pieces, -0.22, 0.18) * array
    return jnp.clip(array, min=-most, max=most).astype(held_as)


def setup_inputs(seed: int = 0) -> dict:
    streams_of = jax.random.split(jax.random.key(seed), 8)
    sources = normal_values(streams_of[0], (TIME_SLICES, STEPS, SUBCIRCUIT_COUNT, SCEN, CIRCUIT_NODES), 1.0, 6.0, ((0, 64), (2, 8)))
    block_inverse = draw_block_inverse(jax.random.fold_in(streams_of[7], 71), 0)
    memory_factor = jnp.clip(jnp.exp(math.log(1.0) - 0.6931472 * jax.random.uniform(streams_of[2], (TIME_SLICES, SUBCIRCUIT_COUNT, CIRCUIT_NODES), jnp.float32) ** level_of(streams_of[2], (TIME_SLICES, SUBCIRCUIT_COUNT, CIRCUIT_NODES), ((0, 64), (1, 8)), -0.2, 0.2)), 0.5, 1.0)
    coupling_target = draw_coupling_target(jax.random.fold_in(streams_of[7], 71), 0)
    coupling_weight = normal_values(streams_of[4], (SUBCIRCUIT_COUNT, KC, PORTS, CIRCUIT_NODES), (4 * CIRCUIT_NODES) ** -0.5, 0.09375, ((0, 8),))
    coarse_decay = draw_coarse_decay(jax.random.fold_in(streams_of[7], 71), 0)
    initial_state = normal_values(streams_of[6], (SUBCIRCUIT_COUNT, SCEN, CIRCUIT_NODES), 1.0, 6.0, ((0, 8),), jnp.float32)
    return {"sources": sources, "block_inverse": block_inverse, "memory_factor": memory_factor, "coupling_target": coupling_target, "coupling_weight": coupling_weight, "coarse_decay": coarse_decay, "initial_state": initial_state}


highest = lax.Precision.HIGHEST


def to_low(values):
    return lax.optimization_barrier(values.astype(jnp.bfloat16)).astype(jnp.float32)


def run_chain(decay_rate, coarse_terms, initial):
    def advance(carried, paired):
        rate_now, extra_term = paired
        return rate_now[:, None, :] * carried + extra_term, carried

    unused, starts = lax.scan(advance, initial, (decay_rate, coarse_terms))
    return starts


def coupling_inflow(wave_now, coupling_target, weights_wide):
    wave_low = to_low(wave_now)
    contrib = jnp.einsum('skpn,tsqn->sktqp', weights_wide, wave_low, precision=highest)
    owners = (coupling_target[:, :, None] == jnp.arange(SUBCIRCUIT_COUNT, dtype=jnp.int32)[None, None, :]).astype(jnp.float32)
    grouped = contrib.reshape((N_CIRC, SUB_DEV) + contrib.shape[1:])
    owner_groups = owners.reshape((N_CIRC, SUB_DEV) + owners.shape[1:])
    partial_sums = jnp.einsum('dskg,dsktqp->dgtqp', owner_groups, grouped, precision=highest)
    return jnp.sum(partial_sums, axis=0)


def fine_slice(begin_state, slice_sources, factor, block_wide, coupling_target, weights_wide):
    wave_now = jnp.broadcast_to(begin_state, (STEPS,) + begin_state.shape)
    for sweep_index in range(SWEEPS):
        inflow = coupling_inflow(wave_now, coupling_target, weights_wide)
        previous = begin_state
        columns = []
        for step_index in range(STEPS):
            drive_term = factor[:, None, :] * previous + slice_sources[step_index].astype(jnp.float32)
            drive_term = drive_term.at[:, :, :PORTS].add(inflow[:, step_index])
            previous = jnp.einsum('smn,sqn->sqm', block_wide, to_low(drive_term), precision=highest)
            columns.append(previous)
        wave_now = jnp.stack(columns)
    return wave_now


def reference(sources, block_inverse, memory_factor, coupling_target, coupling_weight, coarse_decay, initial_state):
    block_wide = block_inverse.astype(jnp.float32)
    weights_wide = coupling_weight.astype(jnp.float32)
    coarse_load = jnp.mean(sources.astype(jnp.float32), axis=1)
    begin_all = run_chain(coarse_decay, coarse_load, initial_state)
    waves = None
    for iteration in range(ITERS):
        def one_slice(packed):
            begin_state, slice_sources, factor = packed
            return fine_slice(begin_state, slice_sources, factor, block_wide, coupling_target, weights_wide)

        waves = lax.map(one_slice, (begin_all, sources, memory_factor))
        correction = waves[:, -1] - coarse_decay[:, :, None, :] * begin_all
        begin_all = run_chain(coarse_decay, correction, initial_state)
    return begin_all, waves.astype(jnp.bfloat16)
```

```python
import jax
import jax.numpy as jnp
from jax import lax
from jax.experimental import pallas as pl
from jax.experimental.pallas import tpu as pltpu
from jax.sharding import Mesh
from jax.sharding import PartitionSpec as P

ITERS = 2
STEPS = 8
SCEN = 16
PORTS = 128
KC = 4
SUBS = 8
LANES = 128
CUTS = ("cuts_0", "cuts_1", "cuts_2")
CIRC = ("circ_0", "circ_1")
F32 = jnp.float32
BF16 = jnp.bfloat16
VMEM = pl.BlockSpec(memory_space=pltpu.VMEM)
SMEM = pl.BlockSpec(memory_space=pltpu.SMEM)


def shape(dims, dtype=F32):
    return jax.ShapeDtypeStruct(dims, dtype)


def call(body, outs, args, name, flops=0, scratch=()):
    specs = [SMEM if a.dtype == jnp.int32 else VMEM for a in args]
    size = sum(a.size * a.dtype.itemsize for a in (*args, *outs))
    return pl.pallas_call(
        body,
        out_shape=outs,
        in_specs=specs,
        out_specs=[VMEM] * len(outs),
        scratch_shapes=list(scratch),
        compiler_params=pltpu.CompilerParams(vmem_limit_bytes=32 << 20),
        cost_estimate=pl.CostEstimate(flops=flops, bytes_accessed=size, transcendentals=0),
        name=name,
    )(*args)


def dot(a, b):
    return jnp.dot(a, b, preferred_element_type=F32)


def pack(state, out_ref):
    for b in range(64):
        block, pair = divmod(b, 8)
        out_ref[b, 0:2, :] = state[2 * pair : 2 * pair + 2, block * LANES : (block + 1) * LANES]


def load_body(sources_ref, decay_ref, out_ref):
    total = sources_ref[0].astype(F32)
    for t in range(1, STEPS):
        total = total + sources_ref[t].astype(F32)
    pack(total * (1.0 / STEPS), out_ref)
    for b in range(64):
        block = b // 8
        row = decay_ref[:, block * LANES : (block + 1) * LANES]
        out_ref[b, 2:4, :] = jnp.concatenate([row, row], axis=0)


def setup_body(b_ref, c_ref, m_ref, bt_ref, ct_ref, h_ref, ch_ref):
    bt_ref[...] = b_ref[...].T
    ct_ref[...] = c_ref[...].T
    response = bt_ref[0:PORTS, :]
    h_ref[0:PORTS, :] = response
    response = response.astype(F32)
    for k in range(1, STEPS):
        response = dot((m_ref[...] * response).astype(BF16), bt_ref[...])
        h_ref[k * PORTS : (k + 1) * PORTS, :] = response.astype(BF16)
    ch_ref[...] = dot(h_ref[...], ct_ref[...]).astype(BF16)


def first_chain_body(mine_ref, terms_ref, initial_ref, start_ref):
    start = initial_ref[mine_ref[0]]
    for n in range(64):
        start_ref[n] = start
        start = terms_ref[n, 2:4, :] * start + terms_ref[n, 0:2, :]


def chain_body(mine_ref, last_ref, terms_ref, old_ref, initial_ref, start_ref):
    start = initial_ref[mine_ref[0]]
    for n in range(64):
        start_ref[n] = start
        decay = terms_ref[n, 2:4, :]
        start = decay * start + (last_ref[n] - decay * old_ref[n])


def group(target_ref, blocks, out_ref):
    for g in range(SUBS):
        total = None
        for k in range(KC):
            feeds = jnp.where(target_ref[k] == g, F32(1.0), F32(0.0))
            term = feeds * blocks[:, k * PORTS : (k + 1) * PORTS]
            total = term if total is None else total + term
        out_ref[g] = total


def start_body(target_ref, pieces_ref, ct_ref, start_ref, out_ref):
    for b in range(64):
        block, pair = divmod(b, 8)
        start_ref[2 * pair : 2 * pair + 2, block * LANES : (block + 1) * LANES] = pieces_ref[b]
    group(target_ref, dot(start_ref[...].astype(BF16), ct_ref[...]), out_ref)


def free_body(start_ref, sources_ref, m_ref, bt_ref, ct_ref, z_ref, cz_ref, low_ref):
    previous = start_ref[...]
    for t in range(STEPS):
        drive = m_ref[...] * previous + sources_ref[t].astype(F32)
        previous = dot(drive.astype(BF16), bt_ref[...])
        z_ref[t * SCEN : (t + 1) * SCEN, :] = previous
        low_ref[t * SCEN : (t + 1) * SCEN, :] = previous.astype(BF16)
    cz_ref[...] = dot(low_ref[...], ct_ref[...])


def delays(inflow, x_ref):
    for k in range(STEPS):
        columns = slice(k * PORTS, (k + 1) * PORTS)
        if k:
            x_ref[0 : k * SCEN, columns] = jnp.zeros((k * SCEN, PORTS), BF16)
        x_ref[k * SCEN :, columns] = inflow[: (STEPS - k) * SCEN]


def couple_first_body(target_ref, f_ref, cz_ref, ch_ref, out_ref, x_ref):
    inflow = jnp.sum(f_ref[...], axis=0).astype(BF16)
    delays(jnp.concatenate([inflow] * STEPS, axis=0), x_ref)
    group(target_ref, cz_ref[...] + dot(x_ref[...], ch_ref[...]), out_ref)


def couple_body(target_ref, f_ref, cz_ref, ch_ref, out_ref, x_ref):
    delays(jnp.sum(f_ref[...], axis=0).astype(BF16), x_ref)
    group(target_ref, cz_ref[...] + dot(x_ref[...], ch_ref[...]), out_ref)


def last_step_body(f_ref, z_ref, h_ref, out_ref, x_ref):
    inflow = jnp.sum(f_ref[...], axis=0).astype(BF16)
    for k in range(STEPS):
        t = STEPS - 1 - k
        x_ref[:, k * PORTS : (k + 1) * PORTS] = inflow[t * SCEN : (t + 1) * SCEN]
    pack(z_ref[(STEPS - 1) * SCEN :, :] + dot(x_ref[...], h_ref[...]), out_ref)


def wave_body(f_ref, z_ref, h_ref, out_ref, wave_ref, x_ref):
    delays(jnp.sum(f_ref[...], axis=0).astype(BF16), x_ref)
    wave = z_ref[...] + dot(x_ref[...], h_ref[...])
    wave_ref[...] = wave.astype(BF16)
    pack(wave[(STEPS - 1) * SCEN :, :], out_ref)


def over_cuts(pieces):
    return lax.all_to_all(pieces, CUTS, 0, 0, tiled=True)


def over_circ(blocks):
    return lax.all_to_all(blocks, CIRC, 0, 0, tiled=True)


def shards(
    sources,
    block_inverse,
    memory_factor,
    coupling_target,
    coupling_weight,
    coarse_decay,
    initial_state,
):
    nodes = block_inverse.shape[-1]
    rows = STEPS * SCEN
    src = sources.reshape(STEPS, SCEN, nodes)
    inverse = block_inverse.reshape(nodes, nodes)
    weight = coupling_weight.reshape(KC * PORTS, nodes)
    factor = memory_factor.reshape(1, nodes)
    decay = coarse_decay.reshape(1, nodes)
    target = coupling_target.reshape(KC)
    mine = lax.axis_index(CUTS).reshape(1).astype(jnp.int32)
    initial = initial_state.reshape(SCEN, 8, LANES).transpose(1, 0, 2).reshape(64, 2, LANES)

    (loads,) = call(load_body, [shape((64, 4, LANES))], (src, decay), "load")
    terms = over_cuts(loads)
    bt, ct, h, ch = call(
        setup_body,
        [
            shape((nodes, nodes), BF16),
            shape((nodes, KC * PORTS), BF16),
            shape((STEPS * PORTS, nodes), BF16),
            shape((STEPS * PORTS, KC * PORTS), BF16),
        ],
        (inverse, weight, factor),
        "setup",
        flops=2 * nodes * nodes * (7 * PORTS + KC * PORTS),
    )
    (starts,) = call(first_chain_body, [shape((64, 2, LANES))], (mine, terms, initial), "chain")
    wave = None
    for iteration in range(ITERS):
        pieces = over_cuts(starts)
        start, sent = call(
            start_body,
            [shape((SCEN, nodes)), shape((SUBS, SCEN, PORTS))],
            (target, pieces, ct),
            "start",
            flops=2 * SCEN * nodes * KC * PORTS,
        )
        inflow = over_circ(sent)
        z, cz = call(
            free_body,
            [shape((rows, nodes)), shape((rows, KC * PORTS))],
            (start, src, factor, bt, ct),
            "free",
            flops=2 * rows * nodes * (nodes + KC * PORTS),
            scratch=[pltpu.VMEM((rows, nodes), BF16)],
        )
        delayed = [pltpu.VMEM((rows, STEPS * PORTS), BF16)]
        for body in (couple_first_body, couple_body):
            (sent,) = call(
                body,
                [shape((SUBS, rows, PORTS))],
                (target, inflow, cz, ch),
                "couple",
                flops=2 * rows * nodes * KC * PORTS,
                scratch=delayed,
            )
            inflow = over_circ(sent)
        if iteration < ITERS - 1:
            (last,) = call(
                last_step_body,
                [shape((64, 2, LANES))],
                (inflow, z, h),
                "last",
                flops=2 * SCEN * nodes * nodes,
                scratch=[pltpu.VMEM((SCEN, STEPS * PORTS), BF16)],
            )
        else:
            last, wave = call(
                wave_body,
                [shape((64, 2, LANES)), shape((rows, nodes), BF16)],
                (inflow, z, h),
                "wave",
                flops=2 * rows * nodes * nodes,
                scratch=delayed,
            )
        (starts,) = call(
            chain_body,
            [shape((64, 2, LANES))],
            (mine, over_cuts(last), terms, starts, initial),
            "chain",
        )
    pieces = over_cuts(starts)
    start = pieces.reshape(8, SCEN, LANES).transpose(1, 0, 2).reshape(1, 1, SCEN, nodes)
    return start, wave.reshape(1, STEPS, 1, SCEN, nodes)


def solution(mesh):
    finer = Mesh(mesh.devices.reshape(4, 2, 8, 4, 2), CUTS + CIRC)
    in_specs = (
        P(CUTS, None, CIRC, None, None),
        P(CIRC, None, None),
        P(CUTS, CIRC, None),
        P(CIRC, None),
        P(CIRC, None, None, None),
        P(CUTS, CIRC, None),
        P(CIRC, None, None),
    )
    out_specs = (P(CUTS, CIRC, None, None), P(CUTS, None, CIRC, None, None))
    return jax.shard_map(
        shards, mesh=finer, in_specs=in_specs, out_specs=out_specs, check_vma=False
    )
```

```python
import jax
import jax.numpy as jnp
from jax import lax
from jax.experimental import pallas as pl
from jax.experimental.pallas import tpu as pltpu
from jax.sharding import Mesh
from jax.sharding import PartitionSpec as P

ITERS = 2
STEPS = 8
SCEN = 16
PORTS = 128
KC = 4
SUBS = 8
CHIPS = 4
LANES = 128
CUTS = ("cuts_0", "cuts_1", "cuts_2")
CIRC = ("circ_0", "circ_1")
F32 = jnp.float32
BF16 = jnp.bfloat16
VMEM = pl.BlockSpec(memory_space=pltpu.VMEM)
HBM = pl.BlockSpec(memory_space=pl.ANY)


def shape(dims, dtype=F32):
    return jax.ShapeDtypeStruct(dims, dtype)


def call(body, outs, args, name, flops=0, scratch=(), place=VMEM, grant=16):
    size = sum(a.size * a.dtype.itemsize for a in (*args, *outs))
    return pl.pallas_call(
        body,
        out_shape=outs,
        in_specs=[place] * len(args),
        out_specs=[VMEM] * len(outs),
        scratch_shapes=list(scratch),
        compiler_params=pltpu.CompilerParams(vmem_limit_bytes=grant << 20),
        cost_estimate=pl.CostEstimate(flops=flops, bytes_accessed=size, transcendentals=0),
        name=name,
    )(*args)


def dot(a, b):
    return jnp.dot(a, b, preferred_element_type=F32)


def pack(state, out_ref):
    for b in range(64):
        block, pair = divmod(b, 8)
        out_ref[b, 0:2, :] = state[2 * pair : 2 * pair + 2, block * LANES : (block + 1) * LANES]


def load_body(sources_ref, decay_ref, out_ref, held_ref, rate_ref, sems):
    rate = pltpu.make_async_copy(decay_ref, rate_ref, sems.at[STEPS])
    steps = [
        pltpu.make_async_copy(sources_ref.at[t], held_ref.at[t], sems.at[t]) for t in range(STEPS)
    ]
    for step in steps:
        step.start()
    rate.start()
    total = None
    for t, step in enumerate(steps):
        step.wait()
        now = held_ref[t].astype(F32)
        total = now if total is None else total + now
    pack(total * (1.0 / STEPS), out_ref)
    rate.wait()
    for b in range(64):
        block = b // 8
        row = rate_ref[:, block * LANES : (block + 1) * LANES]
        out_ref[b, 2:4, :] = jnp.concatenate([row, row], axis=0)


def setup_body(b_ref, c_ref, m_ref, bt_ref, ct_ref, h_ref, ch_ref):
    bt_ref[...] = b_ref[...].T
    ct_ref[...] = c_ref[...].T
    response = bt_ref[0:PORTS, :]
    h_ref[0:PORTS, :] = response
    response = response.astype(F32)
    for k in range(1, STEPS):
        response = dot((m_ref[...] * response).astype(BF16), bt_ref[...])
        h_ref[k * PORTS : (k + 1) * PORTS, :] = response.astype(BF16)
    ch_ref[...] = dot(h_ref[...], ct_ref[...]).astype(BF16)


def first_chain_body(terms_ref, initial_ref, start_ref):
    start = initial_ref[...]
    for n in range(64):
        start_ref[n] = start
        start = terms_ref[n, 2:4, :] * start + terms_ref[n, 0:2, :]


def chain_body(last_ref, terms_ref, old_ref, initial_ref, start_ref):
    start = initial_ref[...]
    for n in range(64):
        start_ref[n] = start
        decay = terms_ref[n, 2:4, :]
        start = decay * start + (last_ref[n] - decay * old_ref[n])


def group(feeds_ref, first, blocks):
    total = None
    for k in range(KC):
        at = first * KC + k
        term = feeds_ref[at : at + 1, :] * blocks[:, k * PORTS : (k + 1) * PORTS]
        total = term if total is None else total + term
    return total


def start_body(feeds_ref, pieces_ref, ct_ref, start_ref, out_ref):
    for b in range(64):
        block, pair = divmod(b, 8)
        start_ref[2 * pair : 2 * pair + 2, block * LANES : (block + 1) * LANES] = pieces_ref[b]
    blocks = dot(start_ref[...].astype(BF16), ct_ref[...])
    for g in range(SUBS):
        out_ref[g] = group(feeds_ref, g, blocks)


def free_body(start_ref, sources_ref, m_ref, bt_ref, ct_ref, z_ref, cz_ref, low_ref):
    previous = start_ref[...]
    for t in range(STEPS):
        drive = m_ref[...] * previous + sources_ref[t].astype(F32)
        previous = dot(drive.astype(BF16), bt_ref[...])
        z_ref[t * SCEN : (t + 1) * SCEN, :] = previous
        low_ref[t * SCEN : (t + 1) * SCEN, :] = previous.astype(BF16)
    cz_ref[...] = dot(low_ref[...], ct_ref[...])


def delays(inflow, x_ref):
    for k in range(STEPS):
        columns = slice(k * PORTS, (k + 1) * PORTS)
        if k:
            x_ref[0 : k * SCEN, columns] = jnp.zeros((k * SCEN, PORTS), BF16)
        x_ref[k * SCEN :, columns] = inflow[: (STEPS - k) * SCEN]


def couple_first_body(feeds_ref, f_ref, cz_ref, ch_ref, blocks_ref, out_ref, x_ref):
    inflow = jnp.sum(f_ref[...], axis=0).astype(BF16)
    delays(jnp.concatenate([inflow] * STEPS, axis=0), x_ref)
    blocks_ref[...] = cz_ref[...] + dot(x_ref[...], ch_ref[...])
    for g in range(CHIPS):
        out_ref[g] = group(feeds_ref, g, blocks_ref[...])


def couple_body(feeds_ref, f_ref, cz_ref, ch_ref, blocks_ref, out_ref, x_ref):
    delays(jnp.sum(f_ref[...], axis=0).astype(BF16), x_ref)
    blocks_ref[...] = cz_ref[...] + dot(x_ref[...], ch_ref[...])
    for g in range(CHIPS):
        out_ref[g] = group(feeds_ref, g, blocks_ref[...])


def gather_body(feeds_ref, blocks_ref, got_ref, out_ref):
    for g in range(CHIPS):
        out_ref[g] = got_ref[g] + group(feeds_ref, g, blocks_ref[...])


def last_step_body(f_ref, z_ref, h_ref, out_ref, x_ref):
    inflow = jnp.sum(f_ref[...], axis=0).astype(BF16)
    for k in range(STEPS):
        t = STEPS - 1 - k
        x_ref[:, k * PORTS : (k + 1) * PORTS] = inflow[t * SCEN : (t + 1) * SCEN]
    pack(z_ref[(STEPS - 1) * SCEN :, :] + dot(x_ref[...], h_ref[...]), out_ref)


def wave_body(f_ref, z_ref, h_ref, out_ref, wave_ref, x_ref):
    delays(jnp.sum(f_ref[...], axis=0).astype(BF16), x_ref)
    wave = z_ref[...] + dot(x_ref[...], h_ref[...])
    wave_ref[...] = wave.astype(BF16)
    pack(wave[(STEPS - 1) * SCEN :, :], out_ref)


def over_cuts(pieces):
    return lax.all_to_all(pieces, CUTS, 0, 0, tiled=True)


def over_circ(blocks):
    return lax.all_to_all(blocks, CIRC, 0, 0, tiled=True)


def over_chips(blocks):
    return lax.all_to_all(blocks, CIRC[0], 0, 0, tiled=True)


def other_core(blocks):
    return lax.ppermute(blocks, CIRC[1], [(0, 1), (1, 0)])


def feeds_of(target, owners):
    feeds = (target[None, :] == owners[:, None]).astype(F32)
    return jnp.broadcast_to(feeds.reshape(-1, 1), (feeds.size, LANES))


def shards(
    sources,
    block_inverse,
    memory_factor,
    coupling_target,
    coupling_weight,
    coarse_decay,
    initial_state,
):
    nodes = block_inverse.shape[-1]
    rows = STEPS * SCEN
    src = sources.reshape(STEPS, SCEN, nodes)
    inverse = block_inverse.reshape(nodes, nodes)
    weight = coupling_weight.reshape(KC * PORTS, nodes)
    factor = memory_factor.reshape(1, nodes)
    decay = coarse_decay.reshape(1, nodes)
    target = coupling_target.reshape(KC)
    core = lax.axis_index(CIRC[1]).astype(jnp.int32)
    chips = 2 * jnp.arange(CHIPS, dtype=jnp.int32)
    feeds_all = feeds_of(target, jnp.arange(SUBS, dtype=jnp.int32))
    feeds_own = feeds_of(target, chips + core)
    feeds_other = feeds_of(target, chips + 1 - core)
    pairs = initial_state.reshape(SCEN, 8, LANES).transpose(1, 0, 2).reshape(64, 2, LANES)
    initial = lax.dynamic_index_in_dim(pairs, lax.axis_index(CUTS), 0, keepdims=False)

    (loads,) = call(
        load_body,
        [shape((64, 4, LANES))],
        (src, decay),
        "load",
        scratch=[
            pltpu.VMEM((STEPS, SCEN, nodes), BF16),
            pltpu.VMEM((1, nodes), F32),
            pltpu.SemaphoreType.DMA((STEPS + 1,)),
        ],
        place=HBM,
        grant=60,
    )
    terms = over_cuts(loads)
    bt, ct, h, ch = call(
        setup_body,
        [
            shape((nodes, nodes), BF16),
            shape((nodes, KC * PORTS), BF16),
            shape((STEPS * PORTS, nodes), BF16),
            shape((STEPS * PORTS, KC * PORTS), BF16),
        ],
        (inverse, weight, factor),
        "setup",
        flops=2 * nodes * nodes * (7 * PORTS + KC * PORTS),
    )
    terms, bt, ct, h, ch = lax.optimization_barrier((terms, bt, ct, h, ch))
    (starts,) = call(first_chain_body, [shape((64, 2, LANES))], (terms, initial), "chain")
    wave = None
    for iteration in range(ITERS):
        pieces = over_cuts(starts)
        start, sent = call(
            start_body,
            [shape((SCEN, nodes)), shape((SUBS, SCEN, PORTS))],
            (feeds_all, pieces, ct),
            "start",
            flops=2 * SCEN * nodes * KC * PORTS,
        )
        inflow = over_circ(sent)
        z, cz = call(
            free_body,
            [shape((rows, nodes)), shape((rows, KC * PORTS))],
            (start, src, factor, bt, ct),
            "free",
            flops=2 * rows * nodes * (nodes + KC * PORTS),
            scratch=[pltpu.VMEM((rows, nodes), BF16)],
        )
        delayed = [pltpu.VMEM((rows, STEPS * PORTS), BF16)]
        for body in (couple_first_body, couple_body):
            blocks, sent = call(
                body,
                [shape((rows, KC * PORTS)), shape((CHIPS, rows, PORTS))],
                (feeds_other, inflow, cz, ch),
                "couple",
                flops=2 * rows * nodes * KC * PORTS,
                scratch=delayed,
            )
            (sent,) = call(
                gather_body,
                [shape((CHIPS, rows, PORTS))],
                (feeds_own, blocks, other_core(sent)),
                "gather",
            )
            inflow = over_chips(sent)
        if iteration < ITERS - 1:
            (last,) = call(
                last_step_body,
                [shape((64, 2, LANES))],
                (inflow, z, h),
                "last",
                flops=2 * SCEN * nodes * nodes,
                scratch=[pltpu.VMEM((SCEN, STEPS * PORTS), BF16)],
            )
        else:
            last, wave = call(
                wave_body,
                [shape((64, 2, LANES)), shape((rows, nodes), BF16)],
                (inflow, z, h),
                "wave",
                flops=2 * rows * nodes * nodes,
                scratch=delayed,
            )
        (starts,) = call(
            chain_body,
            [shape((64, 2, LANES))],
            (over_cuts(last), terms, starts, initial),
            "chain",
        )
    pieces = over_cuts(starts)
    start = pieces.reshape(8, SCEN, LANES).transpose(1, 0, 2).reshape(1, 1, SCEN, nodes)
    return start, wave.reshape(1, STEPS, 1, SCEN, nodes)


def solution(mesh):
    finer = Mesh(mesh.devices.reshape(4, 2, 8, 4, 2), CUTS + CIRC)
    in_specs = (
        P(CUTS, None, CIRC, None, None),
        P(CIRC, None, None),
        P(CUTS, CIRC, None),
        P(CIRC, None),
        P(CIRC, None, None, None),
        P(CUTS, CIRC, None),
        P(CIRC, None, None),
    )
    out_specs = (P(CUTS, CIRC, None, None), P(CUTS, None, CIRC, None, None))
    return jax.shard_map(
        shards, mesh=finer, in_specs=in_specs, out_specs=out_specs, check_vma=False
    )
```

```python
import jax
import jax.numpy as jnp
from jax import lax
from jax.experimental import pallas as pl
from jax.experimental.pallas import tpu as pltpu
from jax.sharding import Mesh
from jax.sharding import PartitionSpec as P

ITERS = 2
STEPS = 8
SCEN = 16
PORTS = 128
KC = 4
SUBS = 8
CHIPS = 4
PARTS = 4
LANES = 128
CUTS = ("cuts_0", "cuts_1", "cuts_2")
CIRC = ("circ_0", "circ_1")
F32 = jnp.float32
BF16 = jnp.bfloat16
VMEM = pl.BlockSpec(memory_space=pltpu.VMEM)
HBM = pl.BlockSpec(memory_space=pl.ANY)


def shape(dims, dtype=F32):
    return jax.ShapeDtypeStruct(dims, dtype)


def call(body, outs, args, name, flops=0, scratch=(), place=VMEM, grant=16, out_places=None):
    size = sum(a.size * a.dtype.itemsize for a in (*args, *outs))
    return pl.pallas_call(
        body,
        out_shape=outs,
        in_specs=[place] * len(args),
        out_specs=out_places or [VMEM] * len(outs),
        scratch_shapes=list(scratch),
        compiler_params=pltpu.CompilerParams(vmem_limit_bytes=grant << 20),
        cost_estimate=pl.CostEstimate(flops=flops, bytes_accessed=size, transcendentals=0),
        name=name,
    )(*args)


def dot(a, b):
    return jnp.dot(a, b, preferred_element_type=F32)


def pack(state, out_ref):
    for b in range(64):
        block, pair = divmod(b, 8)
        out_ref[b, 0:2, :] = state[2 * pair : 2 * pair + 2, block * LANES : (block + 1) * LANES]


def unpack(pieces_ref, state_ref):
    for b in range(64):
        block, pair = divmod(b, 8)
        state_ref[2 * pair : 2 * pair + 2, block * LANES : (block + 1) * LANES] = pieces_ref[b]


def load_body(sources_ref, decay_ref, out_ref, held_ref, rate_ref, sems):
    rate = pltpu.make_async_copy(decay_ref, rate_ref, sems.at[STEPS])
    steps = [
        pltpu.make_async_copy(sources_ref.at[t], held_ref.at[t], sems.at[t]) for t in range(STEPS)
    ]
    for step in steps:
        step.start()
    rate.start()
    total = None
    for t, step in enumerate(steps):
        step.wait()
        now = held_ref[t].astype(F32)
        total = now if total is None else total + now
    pack(total * (1.0 / STEPS), out_ref)
    rate.wait()
    for b in range(64):
        block = b // 8
        row = rate_ref[:, block * LANES : (block + 1) * LANES]
        out_ref[b, 2:4, :] = jnp.concatenate([row, row], axis=0)


def setup_body(
    b_hbm, c_hbm, m_hbm, bt_hbm, ct_ref, h_hbm, ch_ref, b_ref, c_ref, m_ref, bt_ref, h_ref, sems
):
    part = b_ref.shape[0] // PARTS
    rows = [slice(k * part, (k + 1) * part) for k in range(PARTS)]
    parts = [
        pltpu.make_async_copy(b_hbm.at[r], b_ref.at[r], sems.at[k]) for k, r in enumerate(rows)
    ]
    weight = pltpu.make_async_copy(c_hbm, c_ref, sems.at[PARTS])
    factor = pltpu.make_async_copy(m_hbm, m_ref, sems.at[PARTS + 1])
    factor.start()
    for copy in parts:
        copy.start()
    weight.start()
    for r, copy in zip(rows, parts):
        copy.wait()
        bt_ref[:, r] = b_ref[r, :].T
    turned = pltpu.make_async_copy(bt_ref, bt_hbm, sems.at[PARTS + 2])
    turned.start()
    factor.wait()
    response = bt_ref[0:PORTS, :]
    h_ref[0:PORTS, :] = response
    response = response.astype(F32)
    for k in range(1, STEPS):
        response = dot((m_ref[...] * response).astype(BF16), bt_ref[...])
        h_ref[k * PORTS : (k + 1) * PORTS, :] = response.astype(BF16)
    kept = pltpu.make_async_copy(h_ref, h_hbm, sems.at[PARTS + 3])
    kept.start()
    weight.wait()
    ct_ref[...] = c_ref[...].T
    ch_ref[...] = dot(h_ref[...], ct_ref[...]).astype(BF16)
    turned.wait()
    kept.wait()


def first_chain_body(terms_ref, initial_ref, start_ref):
    start = initial_ref[...]
    for n in range(64):
        start_ref[n] = start
        start = terms_ref[n, 2:4, :] * start + terms_ref[n, 0:2, :]


def chain_body(last_ref, terms_ref, old_ref, initial_ref, start_ref):
    start = initial_ref[...]
    for n in range(64):
        start_ref[n] = start
        decay = terms_ref[n, 2:4, :]
        start = decay * start + (last_ref[n] - decay * old_ref[n])


def group(target_ref, first, owner, blocks):
    total = None
    for k in range(KC):
        feeds = target_ref[first + k : first + k + 1, :] == owner
        term = jnp.where(feeds, blocks[:, k * PORTS : (k + 1) * PORTS], F32(0.0))
        total = term if total is None else total + term
    return total


def start_body(target_ref, pieces_ref, ct_ref, start_ref, out_ref):
    unpack(pieces_ref, start_ref)
    blocks = dot(start_ref[...].astype(BF16), ct_ref[...])
    for g in range(SUBS):
        out_ref[g] = group(target_ref, 0, g, blocks)


def free_body(start_ref, sources_ref, m_ref, bt_ref, ct_ref, z_ref, cz_ref, low_ref):
    previous = start_ref[...]
    for t in range(STEPS):
        drive = m_ref[...] * previous + sources_ref[t].astype(F32)
        previous = dot(drive.astype(BF16), bt_ref[...])
        z_ref[t * SCEN : (t + 1) * SCEN, :] = previous
        low_ref[t * SCEN : (t + 1) * SCEN, :] = previous.astype(BF16)
    cz_ref[...] = dot(low_ref[...], ct_ref[...])


def delays(inflow, x_ref):
    for k in range(STEPS):
        columns = slice(k * PORTS, (k + 1) * PORTS)
        if k:
            x_ref[0 : k * SCEN, columns] = jnp.zeros((k * SCEN, PORTS), BF16)
        x_ref[k * SCEN :, columns] = inflow[: (STEPS - k) * SCEN]


def couple_first_body(target_ref, f_ref, cz_ref, ch_ref, blocks_ref, out_ref, x_ref):
    inflow = jnp.sum(f_ref[...], axis=0).astype(BF16)
    delays(jnp.concatenate([inflow] * STEPS, axis=0), x_ref)
    blocks_ref[...] = cz_ref[...] + dot(x_ref[...], ch_ref[...])
    for g in range(CHIPS):
        out_ref[g] = group(target_ref, 2 * KC, 2 * g, blocks_ref[...])


def couple_body(target_ref, f_ref, cz_ref, ch_ref, blocks_ref, out_ref, x_ref):
    delays(jnp.sum(f_ref[...], axis=0).astype(BF16), x_ref)
    blocks_ref[...] = cz_ref[...] + dot(x_ref[...], ch_ref[...])
    for g in range(CHIPS):
        out_ref[g] = group(target_ref, 2 * KC, 2 * g, blocks_ref[...])


def gather_body(target_ref, blocks_ref, got_ref, out_ref):
    for g in range(CHIPS):
        out_ref[g] = got_ref[g] + group(target_ref, KC, 2 * g, blocks_ref[...])


def last_step_body(f_ref, z_ref, h_ref, out_ref, x_ref):
    inflow = jnp.sum(f_ref[...], axis=0).astype(BF16)
    for k in range(STEPS):
        t = STEPS - 1 - k
        x_ref[:, k * PORTS : (k + 1) * PORTS] = inflow[t * SCEN : (t + 1) * SCEN]
    pack(z_ref[(STEPS - 1) * SCEN :, :] + dot(x_ref[...], h_ref[...]), out_ref)


def wave_body(f_ref, z_ref, h_ref, out_ref, wave_ref, x_ref):
    delays(jnp.sum(f_ref[...], axis=0).astype(BF16), x_ref)
    wave = z_ref[...] + dot(x_ref[...], h_ref[...])
    wave_ref[...] = wave.astype(BF16)
    pack(wave[(STEPS - 1) * SCEN :, :], out_ref)


def unpack_body(pieces_ref, state_ref):
    unpack(pieces_ref, state_ref)


def over_cuts(pieces):
    return lax.all_to_all(pieces, CUTS, 0, 0, tiled=True)


def over_circ(blocks):
    return lax.all_to_all(blocks, CIRC, 0, 0, tiled=True)


def over_chips(blocks):
    return lax.all_to_all(blocks, CIRC[0], 0, 0, tiled=True)


def other_core(blocks):
    return lax.ppermute(blocks, CIRC[1], [(0, 1), (1, 0)])


def shards(
    sources,
    block_inverse,
    memory_factor,
    coupling_target,
    coupling_weight,
    coarse_decay,
    initial_state,
):
    nodes = block_inverse.shape[-1]
    rows = STEPS * SCEN
    src = sources.reshape(STEPS, SCEN, nodes)
    inverse = block_inverse.reshape(nodes, nodes)
    weight = coupling_weight.reshape(KC * PORTS, nodes)
    factor = memory_factor.reshape(1, nodes)
    decay = coarse_decay.reshape(1, nodes)
    target = coupling_target.reshape(KC)
    core = lax.axis_index(CIRC[1]).astype(jnp.int32)
    targets = jnp.concatenate([target, target - core, target - (1 - core)])
    targets = jnp.broadcast_to(targets[:, None], (3 * KC, LANES))
    pairs = initial_state.reshape(SCEN, 8, LANES).transpose(1, 0, 2).reshape(64, 2, LANES)
    initial = lax.dynamic_index_in_dim(pairs, lax.axis_index(CUTS), 0, keepdims=False)

    (loads,) = call(
        load_body,
        [shape((64, 4, LANES))],
        (src, decay),
        "load",
        scratch=[
            pltpu.VMEM((STEPS, SCEN, nodes), BF16),
            pltpu.VMEM((1, nodes), F32),
            pltpu.SemaphoreType.DMA((STEPS + 1,)),
        ],
        place=HBM,
        grant=60,
    )
    terms = over_cuts(loads)
    bt, ct, h, ch = call(
        setup_body,
        [
            shape((nodes, nodes), BF16),
            shape((nodes, KC * PORTS), BF16),
            shape((STEPS * PORTS, nodes), BF16),
            shape((STEPS * PORTS, KC * PORTS), BF16),
        ],
        (inverse, weight, factor),
        "setup",
        flops=2 * nodes * nodes * (7 * PORTS + KC * PORTS),
        scratch=[
            pltpu.VMEM((nodes, nodes), BF16),
            pltpu.VMEM((KC * PORTS, nodes), BF16),
            pltpu.VMEM((1, nodes), F32),
            pltpu.VMEM((nodes, nodes), BF16),
            pltpu.VMEM((STEPS * PORTS, nodes), BF16),
            pltpu.SemaphoreType.DMA((PARTS + 4,)),
        ],
        place=HBM,
        grant=56,
        out_places=[HBM, VMEM, HBM, VMEM],
    )
    terms, targets, initial, bt, ct, h, ch = lax.optimization_barrier(
        (terms, targets, initial, bt, ct, h, ch)
    )
    (starts,) = call(first_chain_body, [shape((64, 2, LANES))], (terms, initial), "chain")
    pieces = over_cuts(starts)
    wave = None
    for iteration in range(ITERS):
        start, sent = call(
            start_body,
            [shape((SCEN, nodes)), shape((SUBS, SCEN, PORTS))],
            (targets, pieces, ct),
            "start",
            flops=2 * SCEN * nodes * KC * PORTS,
        )
        inflow = over_circ(sent)
        z, cz = call(
            free_body,
            [shape((rows, nodes)), shape((rows, KC * PORTS))],
            (start, src, factor, bt, ct),
            "free",
            flops=2 * rows * nodes * (nodes + KC * PORTS),
            scratch=[pltpu.VMEM((rows, nodes), BF16)],
        )
        delayed = [pltpu.VMEM((rows, STEPS * PORTS), BF16)]
        for body in (couple_first_body, couple_body):
            blocks, sent = call(
                body,
                [shape((rows, KC * PORTS)), shape((CHIPS, rows, PORTS))],
                (targets, inflow, cz, ch),
                "couple",
                flops=2 * rows * nodes * KC * PORTS,
                scratch=delayed,
            )
            (sent,) = call(
                gather_body,
                [shape((CHIPS, rows, PORTS))],
                (targets, blocks, other_core(sent)),
                "gather",
            )
            inflow = over_chips(sent)
        if iteration < ITERS - 1:
            (last,) = call(
                last_step_body,
                [shape((64, 2, LANES))],
                (inflow, z, h),
                "last",
                flops=2 * SCEN * nodes * nodes,
                scratch=[pltpu.VMEM((SCEN, STEPS * PORTS), BF16)],
            )
        else:
            last, wave = call(
                wave_body,
                [shape((64, 2, LANES)), shape((rows, nodes), BF16)],
                (inflow, z, h),
                "wave",
                flops=2 * rows * nodes * nodes,
                scratch=delayed,
            )
        (starts,) = call(
            chain_body,
            [shape((64, 2, LANES))],
            (over_cuts(last), terms, starts, initial),
            "chain",
        )
        pieces = over_cuts(starts)
    (start,) = call(unpack_body, [shape((SCEN, nodes))], (pieces,), "unpack")
    return start.reshape(1, 1, SCEN, nodes), wave.reshape(1, STEPS, 1, SCEN, nodes)


def solution(mesh):
    finer = Mesh(mesh.devices.reshape(4, 2, 8, 4, 2), CUTS + CIRC)
    in_specs = (
        P(CUTS, None, CIRC, None, None),
        P(CIRC, None, None),
        P(CUTS, CIRC, None),
        P(CIRC, None),
        P(CIRC, None, None, None),
        P(CUTS, CIRC, None),
        P(CIRC, None, None),
    )
    out_specs = (P(CUTS, CIRC, None, None), P(CUTS, None, CIRC, None, None))
    return jax.shard_map(
        shards, mesh=finer, in_specs=in_specs, out_specs=out_specs, check_vma=False
    )
```

```python
import jax
import jax.numpy as jnp
from jax import lax
from jax.experimental import pallas as pl
from jax.experimental.pallas import tpu as pltpu
from jax.sharding import Mesh
from jax.sharding import PartitionSpec as P

ITERS = 2
STEPS = 8
SCEN = 16
PORTS = 128
KC = 4
SUBS = 8
CHIPS = 4
PARTS = 4
GRANT = 50
LANES = 128
CUTS = ("cuts_0", "cuts_1", "cuts_2")
CIRC = ("circ_0", "circ_1")
F32 = jnp.float32
BF16 = jnp.bfloat16
VMEM = pl.BlockSpec(memory_space=pltpu.VMEM)
HBM = pl.BlockSpec(memory_space=pl.ANY)


def shape(dims, dtype=F32):
    return jax.ShapeDtypeStruct(dims, dtype)


def call(body, outs, args, name, flops=0, scratch=(), places=None, grant=16, out_places=None):
    size = sum(a.size * a.dtype.itemsize for a in (*args, *outs))
    return pl.pallas_call(
        body,
        out_shape=outs,
        in_specs=places or [VMEM] * len(args),
        out_specs=out_places or [VMEM] * len(outs),
        scratch_shapes=list(scratch),
        compiler_params=pltpu.CompilerParams(vmem_limit_bytes=grant << 20),
        cost_estimate=pl.CostEstimate(flops=flops, bytes_accessed=size, transcendentals=0),
        name=name,
    )(*args)


def dot(a, b):
    return jnp.dot(a, b, preferred_element_type=F32)


def pack(state, out_ref):
    for b in range(64):
        block, pair = divmod(b, 8)
        out_ref[b, 0:2, :] = state[2 * pair : 2 * pair + 2, block * LANES : (block + 1) * LANES]


def unpack(pieces_ref, state_ref):
    for b in range(64):
        block, pair = divmod(b, 8)
        state_ref[2 * pair : 2 * pair + 2, block * LANES : (block + 1) * LANES] = pieces_ref[b]


def load_body(sources_ref, decay_ref, out_ref, held_ref, rate_ref, sems):
    rate = pltpu.make_async_copy(decay_ref, rate_ref, sems.at[STEPS])
    steps = [
        pltpu.make_async_copy(sources_ref.at[t], held_ref.at[t], sems.at[t]) for t in range(STEPS)
    ]
    for step in steps:
        step.start()
    rate.start()
    total = None
    for t, step in enumerate(steps):
        step.wait()
        now = held_ref[t].astype(F32)
        total = now if total is None else total + now
    pack(total * (1.0 / STEPS), out_ref)
    rate.wait()
    for b in range(64):
        block = b // 8
        row = rate_ref[:, block * LANES : (block + 1) * LANES]
        out_ref[b, 2:4, :] = jnp.concatenate([row, row], axis=0)


def setup_body(
    b_hbm,
    c_hbm,
    target_hbm,
    initial_hbm,
    bt_hbm,
    ct_ref,
    targets_ref,
    initial_ref,
    b_ref,
    c_ref,
    bt_ref,
    target_ref,
    tile_ref,
    sems,
):
    part = b_ref.shape[0] // PARTS
    rows = [slice(k * part, (k + 1) * part) for k in range(PARTS)]
    block, pair = jnp.divmod(lax.axis_index(CUTS), 8)
    tile = initial_hbm.at[
        pl.ds(pl.multiple_of(pair // 4 * 8, 8), 8), pl.ds(pl.multiple_of(block * LANES, LANES), LANES)
    ]
    copies = [
        pltpu.make_async_copy(target_hbm, target_ref, sems.at[0]),
        pltpu.make_async_copy(tile, tile_ref, sems.at[1]),
        pltpu.make_async_copy(c_hbm, c_ref, sems.at[2]),
    ]
    parts = [
        pltpu.make_async_copy(b_hbm.at[r], b_ref.at[r], sems.at[4 + k])
        for k, r in enumerate(rows)
    ]
    for copy in copies + parts:
        copy.start()
    for copy in copies:
        copy.wait()
    core = lax.axis_index(CIRC[1])
    for k in range(KC):
        target = jnp.broadcast_to(target_ref[:, k : k + 1], (1, LANES))
        targets_ref[k : k + 1, :] = target
        targets_ref[KC + k : KC + k + 1, :] = target - core
        targets_ref[2 * KC + k : 2 * KC + k + 1, :] = target - (1 - core)
    initial_ref[...] = tile_ref[pl.ds(pair % 4 * 2, 2), :]
    ct_ref[...] = c_ref[...].T
    for r, copy in zip(rows, parts):
        copy.wait()
        bt_ref[:, r] = b_ref[r, :].T
    turned = pltpu.make_async_copy(bt_ref, bt_hbm, sems.at[3])
    turned.start()
    turned.wait()


def first_chain_body(terms_ref, initial_ref, start_ref):
    start = initial_ref[...]
    for n in range(64):
        start_ref[n] = start
        start = terms_ref[n, 2:4, :] * start + terms_ref[n, 0:2, :]


def chain_body(last_ref, terms_ref, old_ref, initial_ref, start_ref):
    start = initial_ref[...]
    for n in range(64):
        start_ref[n] = start
        decay = terms_ref[n, 2:4, :]
        start = decay * start + (last_ref[n] - decay * old_ref[n])


def group(target_ref, first, owner, blocks):
    total = None
    for k in range(KC):
        feeds = target_ref[first + k : first + k + 1, :] == owner
        term = jnp.where(feeds, blocks[:, k * PORTS : (k + 1) * PORTS], F32(0.0))
        total = term if total is None else total + term
    return total


def start_body(target_ref, pieces_ref, ct_ref, start_ref, out_ref):
    unpack(pieces_ref, start_ref)
    blocks = dot(start_ref[...].astype(BF16), ct_ref[...])
    for g in range(SUBS):
        out_ref[g] = group(target_ref, 0, g, blocks)


def free_body(start_ref, sources_ref, m_ref, bt_ref, ct_ref, z_ref, cz_ref, low_ref):
    previous = start_ref[...]
    for t in range(STEPS):
        drive = m_ref[...] * previous + sources_ref[t].astype(F32)
        previous = dot(drive.astype(BF16), bt_ref[...])
        z_ref[t * SCEN : (t + 1) * SCEN, :] = previous
        low_ref[t * SCEN : (t + 1) * SCEN, :] = previous.astype(BF16)
    cz_ref[...] = dot(low_ref[...], ct_ref[...])


def first_free_body(
    start_ref,
    sources_hbm,
    m_hbm,
    bt_hbm,
    ct_ref,
    z_ref,
    cz_ref,
    h_hbm,
    ch_ref,
    sources_ref,
    m_ref,
    bt_ref,
    h_ref,
    low_ref,
    both_ref,
    sems,
):
    copies = [
        pltpu.make_async_copy(given, taken, sems.at[k])
        for k, (given, taken) in enumerate(
            ((m_hbm, m_ref), (sources_hbm, sources_ref), (bt_hbm, bt_ref))
        )
    ]
    for copy in copies:
        copy.start()
    for copy in copies:
        copy.wait()
    previous = start_ref[...]
    h_ref[0:PORTS, :] = bt_ref[0:PORTS, :]
    response = bt_ref[0:PORTS, :].astype(F32)
    for t in range(STEPS):
        drive = m_ref[...] * previous + sources_ref[t].astype(F32)
        if t == 0:
            previous = dot(drive.astype(BF16), bt_ref[...])
        else:
            both_ref[0:SCEN, :] = drive.astype(BF16)
            both_ref[SCEN:, :] = (m_ref[...] * response).astype(BF16)
            both = dot(both_ref[...], bt_ref[...])
            previous, response = both[:SCEN], both[SCEN:]
            h_ref[t * PORTS : (t + 1) * PORTS, :] = response.astype(BF16)
        z_ref[t * SCEN : (t + 1) * SCEN, :] = previous
        low_ref[t * SCEN : (t + 1) * SCEN, :] = previous.astype(BF16)
    kept = pltpu.make_async_copy(h_ref, h_hbm, sems.at[3])
    kept.start()
    cz_ref[...] = dot(low_ref[...], ct_ref[...])
    ch_ref[...] = dot(h_ref[...], ct_ref[...]).astype(BF16)
    kept.wait()


def delays(inflow, x_ref):
    for k in range(STEPS):
        columns = slice(k * PORTS, (k + 1) * PORTS)
        if k:
            x_ref[0 : k * SCEN, columns] = jnp.zeros((k * SCEN, PORTS), BF16)
        x_ref[k * SCEN :, columns] = inflow[: (STEPS - k) * SCEN]


def couple_first_body(target_ref, f_ref, cz_ref, ch_ref, blocks_ref, out_ref, x_ref):
    inflow = jnp.sum(f_ref[...], axis=0).astype(BF16)
    delays(jnp.concatenate([inflow] * STEPS, axis=0), x_ref)
    blocks_ref[...] = cz_ref[...] + dot(x_ref[...], ch_ref[...])
    for g in range(CHIPS):
        out_ref[g] = group(target_ref, 2 * KC, 2 * g, blocks_ref[...])


def couple_body(target_ref, f_ref, cz_ref, ch_ref, blocks_ref, out_ref, x_ref):
    delays(jnp.sum(f_ref[...], axis=0).astype(BF16), x_ref)
    blocks_ref[...] = cz_ref[...] + dot(x_ref[...], ch_ref[...])
    for g in range(CHIPS):
        out_ref[g] = group(target_ref, 2 * KC, 2 * g, blocks_ref[...])


def gather_body(target_ref, blocks_ref, got_ref, out_ref):
    for g in range(CHIPS):
        out_ref[g] = got_ref[g] + group(target_ref, KC, 2 * g, blocks_ref[...])


def last_step_body(f_ref, z_ref, h_ref, out_ref, x_ref):
    inflow = jnp.sum(f_ref[...], axis=0).astype(BF16)
    for k in range(STEPS):
        t = STEPS - 1 - k
        x_ref[:, k * PORTS : (k + 1) * PORTS] = inflow[t * SCEN : (t + 1) * SCEN]
    pack(z_ref[(STEPS - 1) * SCEN :, :] + dot(x_ref[...], h_ref[...]), out_ref)


def wave_body(f_ref, z_ref, h_ref, out_ref, wave_ref, x_ref):
    delays(jnp.sum(f_ref[...], axis=0).astype(BF16), x_ref)
    wave = z_ref[...] + dot(x_ref[...], h_ref[...])
    wave_ref[...] = wave.astype(BF16)
    pack(wave[(STEPS - 1) * SCEN :, :], out_ref)


def unpack_body(pieces_ref, state_ref):
    unpack(pieces_ref, state_ref)


def over_cuts(pieces):
    return lax.all_to_all(pieces, CUTS, 0, 0, tiled=True)


def over_circ(blocks):
    return lax.all_to_all(blocks, CIRC, 0, 0, tiled=True)


def over_chips(blocks):
    return lax.all_to_all(blocks, CIRC[0], 0, 0, tiled=True)


def other_core(blocks):
    return lax.ppermute(blocks, CIRC[1], [(0, 1), (1, 0)])


def shards(
    sources,
    block_inverse,
    memory_factor,
    coupling_target,
    coupling_weight,
    coarse_decay,
    initial_state,
):
    nodes = block_inverse.shape[-1]
    rows = STEPS * SCEN
    src = sources.reshape(STEPS, SCEN, nodes)
    inverse = block_inverse.reshape(nodes, nodes)
    weight = coupling_weight.reshape(KC * PORTS, nodes)
    factor = memory_factor.reshape(1, nodes)
    decay = coarse_decay.reshape(1, nodes)
    first = initial_state.reshape(SCEN, nodes)
    (loads,) = call(
        load_body,
        [shape((64, 4, LANES))],
        (src, decay),
        "load",
        scratch=[
            pltpu.VMEM((STEPS, SCEN, nodes), BF16),
            pltpu.VMEM((1, nodes), F32),
            pltpu.SemaphoreType.DMA((STEPS + 1,)),
        ],
        places=[HBM] * 2,
        grant=60,
    )
    terms = over_cuts(loads)
    bt, ct, targets, initial = call(
        setup_body,
        [
            shape((nodes, nodes), BF16),
            shape((nodes, KC * PORTS), BF16),
            shape((3 * KC, LANES), jnp.int32),
            shape((2, LANES)),
        ],
        (inverse, weight, coupling_target, first),
        "setup",
        flops=2 * nodes * nodes * SCEN,
        scratch=[
            pltpu.VMEM((nodes, nodes), BF16),
            pltpu.VMEM((KC * PORTS, nodes), BF16),
            pltpu.VMEM((nodes, nodes), BF16),
            pltpu.VMEM((1, KC), jnp.int32),
            pltpu.VMEM((8, LANES), F32),
            pltpu.SemaphoreType.DMA((4 + PARTS,)),
        ],
        places=[HBM] * 4,
        grant=GRANT,
        out_places=[HBM, VMEM, VMEM, VMEM],
    )
    terms, targets, initial, bt, ct = lax.optimization_barrier((terms, targets, initial, bt, ct))
    (starts,) = call(first_chain_body, [shape((64, 2, LANES))], (terms, initial), "chain")
    pieces = over_cuts(starts)
    h = ch = wave = None
    for iteration in range(ITERS):
        start, sent = call(
            start_body,
            [shape((SCEN, nodes)), shape((SUBS, SCEN, PORTS))],
            (targets, pieces, ct),
            "start",
            flops=2 * SCEN * nodes * KC * PORTS,
        )
        inflow = over_circ(sent)
        given = (start, src, factor, bt, ct)
        free = [shape((rows, nodes)), shape((rows, KC * PORTS))]
        low = pltpu.VMEM((rows, nodes), BF16)
        flops = 2 * rows * nodes * (nodes + KC * PORTS)
        if iteration == 0:
            z, cz, h, ch = call(
                first_free_body,
                free
                + [shape((STEPS * PORTS, nodes), BF16), shape((STEPS * PORTS, KC * PORTS), BF16)],
                given,
                "free",
                flops=9 * flops,
                scratch=[
                    pltpu.VMEM((STEPS, SCEN, nodes), BF16),
                    pltpu.VMEM((1, nodes), F32),
                    pltpu.VMEM((nodes, nodes), BF16),
                    pltpu.VMEM((STEPS * PORTS, nodes), BF16),
                    low,
                    pltpu.VMEM((SCEN + PORTS, nodes), BF16),
                    pltpu.SemaphoreType.DMA((4,)),
                ],
                places=[VMEM, HBM, HBM, HBM, VMEM],
                grant=GRANT,
                out_places=[VMEM, VMEM, HBM, VMEM],
            )
        else:
            z, cz = call(free_body, free, given, "free", flops=flops, scratch=[low])
        delayed = [pltpu.VMEM((rows, STEPS * PORTS), BF16)]
        for body in (couple_first_body, couple_body):
            blocks, sent = call(
                body,
                [shape((rows, KC * PORTS)), shape((CHIPS, rows, PORTS))],
                (targets, inflow, cz, ch),
                "couple",
                flops=2 * rows * nodes * KC * PORTS,
                scratch=delayed,
            )
            (sent,) = call(
                gather_body,
                [shape((CHIPS, rows, PORTS))],
                (targets, blocks, other_core(sent)),
                "gather",
            )
            inflow = over_chips(sent)
        if iteration < ITERS - 1:
            (last,) = call(
                last_step_body,
                [shape((64, 2, LANES))],
                (inflow, z, h),
                "last",
                flops=2 * SCEN * nodes * nodes,
                scratch=[pltpu.VMEM((SCEN, STEPS * PORTS), BF16)],
            )
        else:
            last, wave = call(
                wave_body,
                [shape((64, 2, LANES)), shape((rows, nodes), BF16)],
                (inflow, z, h),
                "wave",
                flops=2 * rows * nodes * nodes,
                scratch=delayed,
            )
        (starts,) = call(
            chain_body,
            [shape((64, 2, LANES))],
            (over_cuts(last), terms, starts, initial),
            "chain",
        )
        pieces = over_cuts(starts)
    (start,) = call(unpack_body, [shape((SCEN, nodes))], (pieces,), "unpack")
    return start.reshape(1, 1, SCEN, nodes), wave.reshape(1, STEPS, 1, SCEN, nodes)


def solution(mesh):
    finer = Mesh(mesh.devices.reshape(4, 2, 8, 4, 2), CUTS + CIRC)
    in_specs = (
        P(CUTS, None, CIRC, None, None),
        P(CIRC, None, None),
        P(CUTS, CIRC, None),
        P(CIRC, None),
        P(CIRC, None, None, None),
        P(CUTS, CIRC, None),
        P(CIRC, None, None),
    )
    out_specs = (P(CUTS, CIRC, None, None), P(CUTS, None, CIRC, None, None))
    return jax.shard_map(
        shards, mesh=finer, in_specs=in_specs, out_specs=out_specs, check_vma=False
    )
```

```python
import jax
import jax.numpy as jnp
from jax import lax
from jax.experimental import pallas as pl
from jax.experimental.pallas import tpu as pltpu
from jax.sharding import Mesh
from jax.sharding import PartitionSpec as P

ITERS = 2
STEPS = 8
SCEN = 16
PORTS = 128
KC = 4
SUBS = 8
CHIPS = 4
PARTS = 4
LANES = 128
CUTS = ("cuts_0", "cuts_1", "cuts_2")
CIRC = ("circ_0", "circ_1")
F32 = jnp.float32
BF16 = jnp.bfloat16
VMEM = pl.BlockSpec(memory_space=pltpu.VMEM)
HBM = pl.BlockSpec(memory_space=pl.ANY)


def shape(dims, dtype=F32):
    return jax.ShapeDtypeStruct(dims, dtype)


def call(body, outs, args, name, flops=0, scratch=(), places=None, grant=16, out_places=None):
    size = sum(a.size * a.dtype.itemsize for a in (*args, *outs))
    return pl.pallas_call(
        body,
        out_shape=outs,
        in_specs=places or [VMEM] * len(args),
        out_specs=out_places or [VMEM] * len(outs),
        scratch_shapes=list(scratch),
        compiler_params=pltpu.CompilerParams(vmem_limit_bytes=grant << 20),
        cost_estimate=pl.CostEstimate(flops=flops, bytes_accessed=size, transcendentals=0),
        name=name,
    )(*args)


def dot(a, b):
    return jnp.dot(a, b, preferred_element_type=F32)


def pack(state, out_ref):
    for b in range(64):
        block, pair = divmod(b, 8)
        out_ref[b, 0:2, :] = state[2 * pair : 2 * pair + 2, block * LANES : (block + 1) * LANES]


def unpack(pieces_ref, state_ref):
    for b in range(64):
        block, pair = divmod(b, 8)
        state_ref[2 * pair : 2 * pair + 2, block * LANES : (block + 1) * LANES] = pieces_ref[b]


def load_body(
    sources_ref,
    decay_ref,
    target_hbm,
    initial_hbm,
    out_ref,
    targets_ref,
    initial_ref,
    held_ref,
    rate_ref,
    target_ref,
    tile_ref,
    sems,
):
    block, pair = jnp.divmod(lax.axis_index(CUTS), 8)
    tile = initial_hbm.at[
        pl.ds(pl.multiple_of(pair // 4 * 8, 8), 8), pl.ds(pl.multiple_of(block * LANES, LANES), LANES)
    ]
    steps = [
        pltpu.make_async_copy(sources_ref.at[t], held_ref.at[t], sems.at[t]) for t in range(STEPS)
    ]
    small = [
        pltpu.make_async_copy(given, taken, sems.at[STEPS + k])
        for k, (given, taken) in enumerate(
            ((decay_ref, rate_ref), (target_hbm, target_ref), (tile, tile_ref))
        )
    ]
    for copy in steps + small:
        copy.start()
    total = None
    for t, step in enumerate(steps):
        step.wait()
        now = held_ref[t].astype(F32)
        total = now if total is None else total + now
    pack(total * (1.0 / STEPS), out_ref)
    for copy in small:
        copy.wait()
    for b in range(64):
        block = b // 8
        row = rate_ref[:, block * LANES : (block + 1) * LANES]
        out_ref[b, 2:4, :] = jnp.concatenate([row, row], axis=0)
    core = lax.axis_index(CIRC[1])
    for k in range(KC):
        target = jnp.broadcast_to(target_ref[:, k : k + 1], (1, LANES))
        targets_ref[k : k + 1, :] = target
        targets_ref[KC + k : KC + k + 1, :] = target - core
        targets_ref[2 * KC + k : 2 * KC + k + 1, :] = target - (1 - core)
    initial_ref[...] = tile_ref[pl.ds(pair % 4 * 2, 2), :]


def setup_body(b_hbm, c_hbm, bt_hbm, ct_ref, b_ref, c_ref, bt_ref, sems):
    part = b_ref.shape[0] // PARTS
    rows = [slice(k * part, (k + 1) * part) for k in range(PARTS)]
    weight = pltpu.make_async_copy(c_hbm, c_ref, sems.at[0])
    parts = [
        pltpu.make_async_copy(b_hbm.at[r], b_ref.at[r], sems.at[2 + k])
        for k, r in enumerate(rows)
    ]
    for copy in parts:
        copy.start()
    weight.start()
    for r, copy in zip(rows, parts):
        copy.wait()
        bt_ref[:, r] = b_ref[r, :].T
    turned = pltpu.make_async_copy(bt_ref, bt_hbm, sems.at[1])
    turned.start()
    weight.wait()
    ct_ref[...] = c_ref[...].T
    turned.wait()


def first_chain_body(terms_ref, initial_ref, start_ref):
    start = initial_ref[...]
    for n in range(64):
        start_ref[n] = start
        start = terms_ref[n, 2:4, :] * start + terms_ref[n, 0:2, :]


def chain_body(last_ref, terms_ref, old_ref, initial_ref, start_ref):
    start = initial_ref[...]
    for n in range(64):
        start_ref[n] = start
        decay = terms_ref[n, 2:4, :]
        start = decay * start + (last_ref[n] - decay * old_ref[n])


def group(target_ref, first, owner, blocks):
    total = None
    for k in range(KC):
        feeds = target_ref[first + k : first + k + 1, :] == owner
        term = jnp.where(feeds, blocks[:, k * PORTS : (k + 1) * PORTS], F32(0.0))
        total = term if total is None else total + term
    return total


def start_body(target_ref, pieces_ref, ct_ref, start_ref, out_ref):
    unpack(pieces_ref, start_ref)
    blocks = dot(start_ref[...].astype(BF16), ct_ref[...])
    for g in range(SUBS):
        out_ref[g] = group(target_ref, 0, g, blocks)


def free_body(start_ref, sources_ref, m_ref, bt_ref, ct_ref, z_ref, cz_ref, low_ref):
    previous = start_ref[...]
    for t in range(STEPS):
        drive = m_ref[...] * previous + sources_ref[t].astype(F32)
        previous = dot(drive.astype(BF16), bt_ref[...])
        z_ref[t * SCEN : (t + 1) * SCEN, :] = previous
        low_ref[t * SCEN : (t + 1) * SCEN, :] = previous.astype(BF16)
    cz_ref[...] = dot(low_ref[...], ct_ref[...])


def first_free_body(
    start_ref,
    sources_hbm,
    m_hbm,
    bt_hbm,
    ct_ref,
    z_ref,
    cz_ref,
    h_hbm,
    ch_ref,
    sources_ref,
    m_ref,
    bt_ref,
    h_ref,
    low_ref,
    both_ref,
    sems,
):
    copies = [
        pltpu.make_async_copy(given, taken, sems.at[k])
        for k, (given, taken) in enumerate(
            ((m_hbm, m_ref), (sources_hbm, sources_ref), (bt_hbm, bt_ref))
        )
    ]
    for copy in copies:
        copy.start()
    for copy in copies:
        copy.wait()
    previous = start_ref[...]
    h_ref[0:PORTS, :] = bt_ref[0:PORTS, :]
    response = bt_ref[0:PORTS, :].astype(F32)
    for t in range(STEPS):
        drive = m_ref[...] * previous + sources_ref[t].astype(F32)
        if t == 0:
            previous = dot(drive.astype(BF16), bt_ref[...])
        else:
            both_ref[0:SCEN, :] = drive.astype(BF16)
            both_ref[SCEN:, :] = (m_ref[...] * response).astype(BF16)
            both = dot(both_ref[...], bt_ref[...])
            previous, response = both[:SCEN], both[SCEN:]
            h_ref[t * PORTS : (t + 1) * PORTS, :] = response.astype(BF16)
        z_ref[t * SCEN : (t + 1) * SCEN, :] = previous
        low_ref[t * SCEN : (t + 1) * SCEN, :] = previous.astype(BF16)
    kept = pltpu.make_async_copy(h_ref, h_hbm, sems.at[3])
    kept.start()
    cz_ref[...] = dot(low_ref[...], ct_ref[...])
    ch_ref[...] = dot(h_ref[...], ct_ref[...]).astype(BF16)
    kept.wait()


def delays(inflow, x_ref):
    for k in range(STEPS):
        columns = slice(k * PORTS, (k + 1) * PORTS)
        if k:
            x_ref[0 : k * SCEN, columns] = jnp.zeros((k * SCEN, PORTS), BF16)
        x_ref[k * SCEN :, columns] = inflow[: (STEPS - k) * SCEN]


def couple_first_body(target_ref, f_ref, cz_ref, ch_ref, blocks_ref, out_ref, x_ref):
    inflow = jnp.sum(f_ref[...], axis=0).astype(BF16)
    delays(jnp.concatenate([inflow] * STEPS, axis=0), x_ref)
    blocks_ref[...] = cz_ref[...] + dot(x_ref[...], ch_ref[...])
    for g in range(CHIPS):
        out_ref[g] = group(target_ref, 2 * KC, 2 * g, blocks_ref[...])


def couple_body(target_ref, f_ref, cz_ref, ch_ref, blocks_ref, out_ref, x_ref):
    delays(jnp.sum(f_ref[...], axis=0).astype(BF16), x_ref)
    blocks_ref[...] = cz_ref[...] + dot(x_ref[...], ch_ref[...])
    for g in range(CHIPS):
        out_ref[g] = group(target_ref, 2 * KC, 2 * g, blocks_ref[...])


def gather_body(target_ref, blocks_ref, got_ref, out_ref):
    for g in range(CHIPS):
        out_ref[g] = got_ref[g] + group(target_ref, KC, 2 * g, blocks_ref[...])


def last_step_body(f_ref, z_ref, h_ref, out_ref, x_ref):
    inflow = jnp.sum(f_ref[...], axis=0).astype(BF16)
    for k in range(STEPS):
        t = STEPS - 1 - k
        x_ref[:, k * PORTS : (k + 1) * PORTS] = inflow[t * SCEN : (t + 1) * SCEN]
    pack(z_ref[(STEPS - 1) * SCEN :, :] + dot(x_ref[...], h_ref[...]), out_ref)


def wave_body(f_ref, z_ref, h_ref, out_ref, wave_ref, x_ref):
    delays(jnp.sum(f_ref[...], axis=0).astype(BF16), x_ref)
    wave = z_ref[...] + dot(x_ref[...], h_ref[...])
    wave_ref[...] = wave.astype(BF16)
    pack(wave[(STEPS - 1) * SCEN :, :], out_ref)


def unpack_body(pieces_ref, state_ref):
    unpack(pieces_ref, state_ref)


def over_cuts(pieces):
    return lax.all_to_all(pieces, CUTS, 0, 0, tiled=True)


def over_circ(blocks):
    return lax.all_to_all(blocks, CIRC, 0, 0, tiled=True)


def over_chips(blocks):
    return lax.all_to_all(blocks, CIRC[0], 0, 0, tiled=True)


def other_core(blocks):
    return lax.ppermute(blocks, CIRC[1], [(0, 1), (1, 0)])


def shards(
    sources,
    block_inverse,
    memory_factor,
    coupling_target,
    coupling_weight,
    coarse_decay,
    initial_state,
):
    nodes = block_inverse.shape[-1]
    rows = STEPS * SCEN
    src = sources.reshape(STEPS, SCEN, nodes)
    inverse = block_inverse.reshape(nodes, nodes)
    weight = coupling_weight.reshape(KC * PORTS, nodes)
    factor = memory_factor.reshape(1, nodes)
    decay = coarse_decay.reshape(1, nodes)
    first = initial_state.reshape(SCEN, nodes)
    loads, targets, initial = call(
        load_body,
        [shape((64, 4, LANES)), shape((3 * KC, LANES), jnp.int32), shape((2, LANES))],
        (src, decay, coupling_target, first),
        "load",
        scratch=[
            pltpu.VMEM((STEPS, SCEN, nodes), BF16),
            pltpu.VMEM((1, nodes), F32),
            pltpu.VMEM((1, KC), jnp.int32),
            pltpu.VMEM((8, LANES), F32),
            pltpu.SemaphoreType.DMA((STEPS + 3,)),
        ],
        places=[HBM] * 4,
        grant=60,
    )
    terms = over_cuts(loads)
    bt, ct = call(
        setup_body,
        [shape((nodes, nodes), BF16), shape((nodes, KC * PORTS), BF16)],
        (inverse, weight),
        "setup",
        flops=2 * nodes * nodes * SCEN,
        scratch=[
            pltpu.VMEM((nodes, nodes), BF16),
            pltpu.VMEM((KC * PORTS, nodes), BF16),
            pltpu.VMEM((nodes, nodes), BF16),
            pltpu.SemaphoreType.DMA((2 + PARTS,)),
        ],
        places=[HBM] * 2,
        grant=52,
        out_places=[HBM, VMEM],
    )
    terms, bt, ct = lax.optimization_barrier((terms, bt, ct))
    (starts,) = call(first_chain_body, [shape((64, 2, LANES))], (terms, initial), "chain")
    pieces = over_cuts(starts)
    h = ch = wave = None
    for iteration in range(ITERS):
        start, sent = call(
            start_body,
            [shape((SCEN, nodes)), shape((SUBS, SCEN, PORTS))],
            (targets, pieces, ct),
            "start",
            flops=2 * SCEN * nodes * KC * PORTS,
        )
        inflow = over_circ(sent)
        given = (start, src, factor, bt, ct)
        free = [shape((rows, nodes)), shape((rows, KC * PORTS))]
        low = pltpu.VMEM((rows, nodes), BF16)
        flops = 2 * rows * nodes * (nodes + KC * PORTS)
        if iteration == 0:
            z, cz, h, ch = call(
                first_free_body,
                free
                + [shape((STEPS * PORTS, nodes), BF16), shape((STEPS * PORTS, KC * PORTS), BF16)],
                given,
                "free",
                flops=9 * flops,
                scratch=[
                    pltpu.VMEM((STEPS, SCEN, nodes), BF16),
                    pltpu.VMEM((1, nodes), F32),
                    pltpu.VMEM((nodes, nodes), BF16),
                    pltpu.VMEM((STEPS * PORTS, nodes), BF16),
                    low,
                    pltpu.VMEM((SCEN + PORTS, nodes), BF16),
                    pltpu.SemaphoreType.DMA((4,)),
                ],
                places=[VMEM, HBM, HBM, HBM, VMEM],
                grant=50,
                out_places=[VMEM, VMEM, HBM, VMEM],
            )
        else:
            z, cz = call(free_body, free, given, "free", flops=flops, scratch=[low])
        delayed = [pltpu.VMEM((rows, STEPS * PORTS), BF16)]
        for body in (couple_first_body, couple_body):
            blocks, sent = call(
                body,
                [shape((rows, KC * PORTS)), shape((CHIPS, rows, PORTS))],
                (targets, inflow, cz, ch),
                "couple",
                flops=2 * rows * nodes * KC * PORTS,
                scratch=delayed,
            )
            (sent,) = call(
                gather_body,
                [shape((CHIPS, rows, PORTS))],
                (targets, blocks, other_core(sent)),
                "gather",
            )
            inflow = over_chips(sent)
        if iteration < ITERS - 1:
            (last,) = call(
                last_step_body,
                [shape((64, 2, LANES))],
                (inflow, z, h),
                "last",
                flops=2 * SCEN * nodes * nodes,
                scratch=[pltpu.VMEM((SCEN, STEPS * PORTS), BF16)],
            )
        else:
            last, wave = call(
                wave_body,
                [shape((64, 2, LANES)), shape((rows, nodes), BF16)],
                (inflow, z, h),
                "wave",
                flops=2 * rows * nodes * nodes,
                scratch=delayed,
            )
        (starts,) = call(
            chain_body,
            [shape((64, 2, LANES))],
            (over_cuts(last), terms, starts, initial),
            "chain",
        )
        pieces = over_cuts(starts)
    (start,) = call(unpack_body, [shape((SCEN, nodes))], (pieces,), "unpack")
    return start.reshape(1, 1, SCEN, nodes), wave.reshape(1, STEPS, 1, SCEN, nodes)


def solution(mesh):
    finer = Mesh(mesh.devices.reshape(4, 2, 8, 4, 2), CUTS + CIRC)
    in_specs = (
        P(CUTS, None, CIRC, None, None),
        P(CIRC, None, None),
        P(CUTS, CIRC, None),
        P(CIRC, None),
        P(CIRC, None, None, None),
        P(CUTS, CIRC, None),
        P(CIRC, None, None),
    )
    out_specs = (P(CUTS, CIRC, None, None), P(CUTS, None, CIRC, None, None))
    return jax.shard_map(
        shards, mesh=finer, in_specs=in_specs, out_specs=out_specs, check_vma=False
    )
```

```python
import jax
import jax.numpy as jnp
from jax import lax
from jax.experimental import pallas as pl
from jax.experimental.pallas import tpu as pltpu
from jax.sharding import Mesh
from jax.sharding import PartitionSpec as P

ITERS = 2
STEPS = 8
SCEN = 16
PORTS = 128
KC = 4
SUBS = 8
CHIPS = 4
PARTS = 4
LANES = 128
CUTS = ("cuts_0", "cuts_1", "cuts_2")
CIRC = ("circ_0", "circ_1")
F32 = jnp.float32
BF16 = jnp.bfloat16
VMEM = pl.BlockSpec(memory_space=pltpu.VMEM)
HBM = pl.BlockSpec(memory_space=pl.ANY)


def shape(dims, dtype=F32):
    return jax.ShapeDtypeStruct(dims, dtype)


def call(body, outs, args, name, flops=0, scratch=(), places=None, grant=16, out_places=None):
    size = sum(a.size * a.dtype.itemsize for a in (*args, *outs))
    return pl.pallas_call(
        body,
        out_shape=outs,
        in_specs=places or [VMEM] * len(args),
        out_specs=out_places or [VMEM] * len(outs),
        scratch_shapes=list(scratch),
        compiler_params=pltpu.CompilerParams(vmem_limit_bytes=grant << 20),
        cost_estimate=pl.CostEstimate(flops=flops, bytes_accessed=size, transcendentals=0),
        name=name,
    )(*args)


def dot(a, b):
    return jnp.dot(a, b, preferred_element_type=F32)


def pack(state, out_ref, first=0):
    for b in range(state.shape[1] // LANES * 8):
        block, pair = divmod(b, 8)
        out_ref[first * 8 + b, 0:2, :] = state[
            2 * pair : 2 * pair + 2, block * LANES : (block + 1) * LANES
        ]


def unpack(pieces_ref, state_ref):
    for b in range(64):
        block, pair = divmod(b, 8)
        state_ref[2 * pair : 2 * pair + 2, block * LANES : (block + 1) * LANES] = pieces_ref[b]


def load_body(
    sources_ref,
    decay_ref,
    target_hbm,
    initial_hbm,
    out_ref,
    targets_ref,
    initial_ref,
    held_ref,
    rate_ref,
    target_ref,
    tile_ref,
    sems,
):
    block, pair = jnp.divmod(lax.axis_index(CUTS), 8)
    tile = initial_hbm.at[
        pl.ds(pl.multiple_of(pair // 4 * 8, 8), 8), pl.ds(pl.multiple_of(block * LANES, LANES), LANES)
    ]
    steps = [
        pltpu.make_async_copy(sources_ref.at[t], held_ref.at[t], sems.at[t]) for t in range(STEPS)
    ]
    small = [
        pltpu.make_async_copy(given, taken, sems.at[STEPS + k])
        for k, (given, taken) in enumerate(
            ((decay_ref, rate_ref), (target_hbm, target_ref), (tile, tile_ref))
        )
    ]
    for copy in steps + small:
        copy.start()
    total = None
    for t, step in enumerate(steps):
        step.wait()
        now = held_ref[t].astype(F32)
        total = now if total is None else total + now
    pack(total * (1.0 / STEPS), out_ref)
    for copy in small:
        copy.wait()
    for b in range(64):
        block = b // 8
        row = rate_ref[:, block * LANES : (block + 1) * LANES]
        out_ref[b, 2:4, :] = jnp.concatenate([row, row], axis=0)
    core = lax.axis_index(CIRC[1])
    for k in range(KC):
        target = jnp.broadcast_to(target_ref[:, k : k + 1], (1, LANES))
        targets_ref[k : k + 1, :] = target
        targets_ref[KC + k : KC + k + 1, :] = target - core
        targets_ref[2 * KC + k : 2 * KC + k + 1, :] = target - (1 - core)
    initial_ref[...] = tile_ref[pl.ds(pair % 4 * 2, 2), :]


def setup_body(b_hbm, c_hbm, bt_hbm, ct_ref, b_ref, c_ref, bt_ref, sems):
    part = b_ref.shape[0] // PARTS
    rows = [slice(k * part, (k + 1) * part) for k in range(PARTS)]
    weight = pltpu.make_async_copy(c_hbm, c_ref, sems.at[0])
    parts = [
        pltpu.make_async_copy(b_hbm.at[r], b_ref.at[r], sems.at[2 + k])
        for k, r in enumerate(rows)
    ]
    for copy in parts:
        copy.start()
    weight.start()
    for r, copy in zip(rows, parts):
        copy.wait()
        bt_ref[:, r] = b_ref[r, :].T
    turned = pltpu.make_async_copy(bt_ref, bt_hbm, sems.at[1])
    turned.start()
    weight.wait()
    ct_ref[...] = c_ref[...].T
    turned.wait()


def first_chain_body(terms_ref, initial_ref, start_ref):
    start = initial_ref[...]
    for n in range(64):
        start_ref[n] = start
        start = terms_ref[n, 2:4, :] * start + terms_ref[n, 0:2, :]


def chain_body(last_ref, terms_ref, old_ref, initial_ref, start_ref):
    start = initial_ref[...]
    for n in range(64):
        start_ref[n] = start
        decay = terms_ref[n, 2:4, :]
        start = decay * start + (last_ref[n] - decay * old_ref[n])


def group(target_ref, first, owner, blocks):
    total = None
    for k in range(KC):
        feeds = target_ref[first + k : first + k + 1, :] == owner
        term = jnp.where(feeds, blocks[:, k * PORTS : (k + 1) * PORTS], F32(0.0))
        total = term if total is None else total + term
    return total


def start_body(target_ref, pieces_ref, ct_ref, start_ref, out_ref):
    unpack(pieces_ref, start_ref)
    blocks = dot(start_ref[...].astype(BF16), ct_ref[...])
    for g in range(SUBS):
        out_ref[g] = group(target_ref, 0, g, blocks)


def free_body(start_ref, sources_ref, m_ref, bt_ref, ct_ref, z_ref, cz_ref, low_ref):
    previous = start_ref[...]
    for t in range(STEPS):
        drive = m_ref[...] * previous + sources_ref[t].astype(F32)
        previous = dot(drive.astype(BF16), bt_ref[...])
        z_ref[t * SCEN : (t + 1) * SCEN, :] = previous
        low_ref[t * SCEN : (t + 1) * SCEN, :] = previous.astype(BF16)
    cz_ref[...] = dot(low_ref[...], ct_ref[...])


def first_free_body(
    start_ref,
    sources_hbm,
    m_hbm,
    bt_hbm,
    ct_ref,
    z_ref,
    cz_ref,
    h_hbm,
    ch_ref,
    sources_ref,
    m_ref,
    bt_ref,
    h_ref,
    low_ref,
    both_ref,
    sems,
):
    part = bt_ref.shape[0] // PARTS
    rows = [slice(k * part, (k + 1) * part) for k in range(PARTS)]
    copies = [
        pltpu.make_async_copy(given, taken, sems.at[1 + k])
        for k, (given, taken) in enumerate(((m_hbm, m_ref), (sources_hbm, sources_ref)))
    ]
    parts = [
        pltpu.make_async_copy(bt_hbm.at[r], bt_ref.at[r], sems.at[3 + k])
        for k, r in enumerate(rows)
    ]
    for copy in copies + parts:
        copy.start()
    for copy in copies:
        copy.wait()
    previous = start_ref[...]
    for t in range(STEPS):
        drive = m_ref[...] * previous + sources_ref[t].astype(F32)
        if t == 0:
            drive = drive.astype(BF16)
            previous = jnp.zeros_like(previous)
            for r, copy in zip(rows, parts):
                copy.wait()
                previous = previous + dot(drive[:, r], bt_ref[r, :])
            response = bt_ref[0:PORTS, :]
            h_ref[0:PORTS, :] = response
            response = response.astype(F32)
        else:
            both_ref[0:SCEN, :] = drive.astype(BF16)
            both_ref[SCEN:, :] = (m_ref[...] * response).astype(BF16)
            both = dot(both_ref[...], bt_ref[...])
            previous, response = both[:SCEN], both[SCEN:]
            h_ref[t * PORTS : (t + 1) * PORTS, :] = response.astype(BF16)
        z_ref[t * SCEN : (t + 1) * SCEN, :] = previous
        low_ref[t * SCEN : (t + 1) * SCEN, :] = previous.astype(BF16)
    kept = pltpu.make_async_copy(h_ref, h_hbm, sems.at[0])
    kept.start()
    cz_ref[...] = dot(low_ref[...], ct_ref[...])
    ch_ref[...] = dot(h_ref[...], ct_ref[...]).astype(BF16)
    kept.wait()


def delays(inflow, x_ref):
    for k in range(STEPS):
        columns = slice(k * PORTS, (k + 1) * PORTS)
        if k:
            x_ref[0 : k * SCEN, columns] = jnp.zeros((k * SCEN, PORTS), BF16)
        x_ref[k * SCEN :, columns] = inflow[: (STEPS - k) * SCEN]


def couple_first_body(target_ref, f_ref, cz_ref, ch_ref, blocks_ref, out_ref, x_ref):
    inflow = jnp.sum(f_ref[...], axis=0).astype(BF16)
    delays(jnp.concatenate([inflow] * STEPS, axis=0), x_ref)
    blocks_ref[...] = cz_ref[...] + dot(x_ref[...], ch_ref[...])
    for g in range(CHIPS):
        out_ref[g] = group(target_ref, 2 * KC, 2 * g, blocks_ref[...])


def couple_body(target_ref, f_ref, cz_ref, ch_ref, blocks_ref, out_ref, x_ref):
    delays(jnp.sum(f_ref[...], axis=0).astype(BF16), x_ref)
    blocks_ref[...] = cz_ref[...] + dot(x_ref[...], ch_ref[...])
    for g in range(CHIPS):
        out_ref[g] = group(target_ref, 2 * KC, 2 * g, blocks_ref[...])


def gather_body(target_ref, blocks_ref, got_ref, out_ref):
    for g in range(CHIPS):
        out_ref[g] = got_ref[g] + group(target_ref, KC, 2 * g, blocks_ref[...])


def last_step_body(f_ref, z_ref, h_ref, out_ref, x_ref):
    inflow = jnp.sum(f_ref[...], axis=0).astype(BF16)
    for k in range(STEPS):
        t = STEPS - 1 - k
        x_ref[:, k * PORTS : (k + 1) * PORTS] = inflow[t * SCEN : (t + 1) * SCEN]
    pack(z_ref[(STEPS - 1) * SCEN :, :] + dot(x_ref[...], h_ref[...]), out_ref)


def wave_body(f_ref, z_ref, h_ref, out_ref, wave_hbm, wave_ref, x_ref, sems):
    delays(jnp.sum(f_ref[...], axis=0).astype(BF16), x_ref)
    part = wave_ref.shape[1] // PARTS
    copies = []
    for k in range(PARTS):
        columns = slice(k * part, (k + 1) * part)
        wave = z_ref[:, columns] + dot(x_ref[...], h_ref[:, columns])
        wave_ref[:, columns] = wave.astype(BF16)
        copies.append(
            pltpu.make_async_copy(wave_ref.at[:, columns], wave_hbm.at[:, columns], sems.at[k])
        )
        copies[-1].start()
        pack(wave[(STEPS - 1) * SCEN :, :], out_ref, k * part // LANES)
    for copy in copies:
        copy.wait()


def unpack_body(pieces_ref, state_ref):
    unpack(pieces_ref, state_ref)


def over_cuts(pieces):
    return lax.all_to_all(pieces, CUTS, 0, 0, tiled=True)


def over_circ(blocks):
    return lax.all_to_all(blocks, CIRC, 0, 0, tiled=True)


def over_chips(blocks):
    return lax.all_to_all(blocks, CIRC[0], 0, 0, tiled=True)


def other_core(blocks):
    return lax.ppermute(blocks, CIRC[1], [(0, 1), (1, 0)])


def shards(
    sources,
    block_inverse,
    memory_factor,
    coupling_target,
    coupling_weight,
    coarse_decay,
    initial_state,
):
    nodes = block_inverse.shape[-1]
    rows = STEPS * SCEN
    src = sources.reshape(STEPS, SCEN, nodes)
    inverse = block_inverse.reshape(nodes, nodes)
    weight = coupling_weight.reshape(KC * PORTS, nodes)
    factor = memory_factor.reshape(1, nodes)
    decay = coarse_decay.reshape(1, nodes)
    first = initial_state.reshape(SCEN, nodes)
    loads, targets, initial = call(
        load_body,
        [shape((64, 4, LANES)), shape((3 * KC, LANES), jnp.int32), shape((2, LANES))],
        (src, decay, coupling_target, first),
        "load",
        scratch=[
            pltpu.VMEM((STEPS, SCEN, nodes), BF16),
            pltpu.VMEM((1, nodes), F32),
            pltpu.VMEM((1, KC), jnp.int32),
            pltpu.VMEM((8, LANES), F32),
            pltpu.SemaphoreType.DMA((STEPS + 3,)),
        ],
        places=[HBM] * 4,
        grant=60,
    )
    terms = over_cuts(loads)
    bt, ct = call(
        setup_body,
        [shape((nodes, nodes), BF16), shape((nodes, KC * PORTS), BF16)],
        (inverse, weight),
        "setup",
        flops=2 * nodes * nodes * SCEN,
        scratch=[
            pltpu.VMEM((nodes, nodes), BF16),
            pltpu.VMEM((KC * PORTS, nodes), BF16),
            pltpu.VMEM((nodes, nodes), BF16),
            pltpu.SemaphoreType.DMA((2 + PARTS,)),
        ],
        places=[HBM] * 2,
        grant=52,
        out_places=[HBM, VMEM],
    )
    terms, bt, ct = lax.optimization_barrier((terms, bt, ct))
    (starts,) = call(first_chain_body, [shape((64, 2, LANES))], (terms, initial), "chain")
    pieces = over_cuts(starts)
    h = ch = wave = None
    for iteration in range(ITERS):
        start, sent = call(
            start_body,
            [shape((SCEN, nodes)), shape((SUBS, SCEN, PORTS))],
            (targets, pieces, ct),
            "start",
            flops=2 * SCEN * nodes * KC * PORTS,
        )
        inflow = over_circ(sent)
        given = (start, src, factor, bt, ct)
        free = [shape((rows, nodes)), shape((rows, KC * PORTS))]
        low = pltpu.VMEM((rows, nodes), BF16)
        flops = 2 * rows * nodes * (nodes + KC * PORTS)
        if iteration == 0:
            z, cz, h, ch = call(
                first_free_body,
                free
                + [shape((STEPS * PORTS, nodes), BF16), shape((STEPS * PORTS, KC * PORTS), BF16)],
                given,
                "free",
                flops=9 * flops,
                scratch=[
                    pltpu.VMEM((STEPS, SCEN, nodes), BF16),
                    pltpu.VMEM((1, nodes), F32),
                    pltpu.VMEM((nodes, nodes), BF16),
                    pltpu.VMEM((STEPS * PORTS, nodes), BF16),
                    low,
                    pltpu.VMEM((SCEN + PORTS, nodes), BF16),
                    pltpu.SemaphoreType.DMA((3 + PARTS,)),
                ],
                places=[VMEM, HBM, HBM, HBM, VMEM],
                grant=50,
                out_places=[VMEM, VMEM, HBM, VMEM],
            )
        else:
            z, cz = call(free_body, free, given, "free", flops=flops, scratch=[low])
        delayed = [pltpu.VMEM((rows, STEPS * PORTS), BF16)]
        for body in (couple_first_body, couple_body):
            blocks, sent = call(
                body,
                [shape((rows, KC * PORTS)), shape((CHIPS, rows, PORTS))],
                (targets, inflow, cz, ch),
                "couple",
                flops=2 * rows * nodes * KC * PORTS,
                scratch=delayed,
            )
            (sent,) = call(
                gather_body,
                [shape((CHIPS, rows, PORTS))],
                (targets, blocks, other_core(sent)),
                "gather",
            )
            inflow = over_chips(sent)
        if iteration < ITERS - 1:
            (last,) = call(
                last_step_body,
                [shape((64, 2, LANES))],
                (inflow, z, h),
                "last",
                flops=2 * SCEN * nodes * nodes,
                scratch=[pltpu.VMEM((SCEN, STEPS * PORTS), BF16)],
            )
        else:
            last, wave = call(
                wave_body,
                [shape((64, 2, LANES)), shape((rows, nodes), BF16)],
                (inflow, z, h),
                "wave",
                flops=2 * rows * nodes * nodes,
                scratch=[
                    pltpu.VMEM((rows, nodes), BF16),
                    *delayed,
                    pltpu.SemaphoreType.DMA((PARTS,)),
                ],
                out_places=[VMEM, HBM],
            )
        (starts,) = call(
            chain_body,
            [shape((64, 2, LANES))],
            (over_cuts(last), terms, starts, initial),
            "chain",
        )
        pieces = over_cuts(starts)
    (start,) = call(unpack_body, [shape((SCEN, nodes))], (pieces,), "unpack")
    return start.reshape(1, 1, SCEN, nodes), wave.reshape(1, STEPS, 1, SCEN, nodes)


def solution(mesh):
    finer = Mesh(mesh.devices.reshape(4, 2, 8, 4, 2), CUTS + CIRC)
    in_specs = (
        P(CUTS, None, CIRC, None, None),
        P(CIRC, None, None),
        P(CUTS, CIRC, None),
        P(CIRC, None),
        P(CIRC, None, None, None),
        P(CUTS, CIRC, None),
        P(CIRC, None, None),
    )
    out_specs = (P(CUTS, CIRC, None, None), P(CUTS, None, CIRC, None, None))
    return jax.shard_map(
        shards, mesh=finer, in_specs=in_specs, out_specs=out_specs, check_vma=False
    )
```

```python
import jax
import jax.numpy as jnp
from jax import lax
from jax.experimental import pallas as pl
from jax.experimental.pallas import tpu as pltpu
from jax.sharding import Mesh
from jax.sharding import PartitionSpec as P

ITERS = 2
STEPS = 8
SCEN = 16
PORTS = 128
KC = 4
SUBS = 8
CHIPS = 4
PARTS = 4
LANES = 128
CUTS = ("cuts_0", "cuts_1", "cuts_2")
CIRC = ("circ_0", "circ_1")
F32 = jnp.float32
BF16 = jnp.bfloat16
VMEM = pl.BlockSpec(memory_space=pltpu.VMEM)
HBM = pl.BlockSpec(memory_space=pl.ANY)


def shape(dims, dtype=F32):
    return jax.ShapeDtypeStruct(dims, dtype)


def call(body, outs, args, name, flops=0, scratch=(), places=None, grant=16, out_places=None):
    size = sum(a.size * a.dtype.itemsize for a in (*args, *outs))
    return pl.pallas_call(
        body,
        out_shape=outs,
        in_specs=places or [VMEM] * len(args),
        out_specs=out_places or [VMEM] * len(outs),
        scratch_shapes=list(scratch),
        compiler_params=pltpu.CompilerParams(vmem_limit_bytes=grant << 20),
        cost_estimate=pl.CostEstimate(flops=flops, bytes_accessed=size, transcendentals=0),
        name=name,
    )(*args)


def dot(a, b):
    return jnp.dot(a, b, preferred_element_type=F32)


def pack(state, out_ref, first=0):
    for b in range(state.shape[1] // LANES * 8):
        block, pair = divmod(b, 8)
        out_ref[first * 8 + b, 0:2, :] = state[
            2 * pair : 2 * pair + 2, block * LANES : (block + 1) * LANES
        ]


def unpack(pieces_ref, state_ref):
    for b in range(64):
        block, pair = divmod(b, 8)
        state_ref[2 * pair : 2 * pair + 2, block * LANES : (block + 1) * LANES] = pieces_ref[b]


def load_body(
    sources_ref,
    decay_ref,
    target_hbm,
    initial_hbm,
    out_ref,
    targets_ref,
    initial_ref,
    held_ref,
    rate_ref,
    target_ref,
    tile_ref,
    sems,
):
    block, pair = jnp.divmod(lax.axis_index(CUTS), 8)
    tile = initial_hbm.at[
        pl.ds(pl.multiple_of(pair // 4 * 8, 8), 8), pl.ds(pl.multiple_of(block * LANES, LANES), LANES)
    ]
    steps = [
        pltpu.make_async_copy(sources_ref.at[t], held_ref.at[t], sems.at[t]) for t in range(STEPS)
    ]
    small = [
        pltpu.make_async_copy(given, taken, sems.at[STEPS + k])
        for k, (given, taken) in enumerate(
            ((decay_ref, rate_ref), (target_hbm, target_ref), (tile, tile_ref))
        )
    ]
    for copy in steps + small:
        copy.start()
    total = None
    for t, step in enumerate(steps):
        step.wait()
        now = held_ref[t].astype(F32)
        total = now if total is None else total + now
    pack(total * (1.0 / STEPS), out_ref)
    for copy in small:
        copy.wait()
    for b in range(64):
        block = b // 8
        row = rate_ref[:, block * LANES : (block + 1) * LANES]
        out_ref[b, 2:4, :] = jnp.concatenate([row, row], axis=0)
    core = lax.axis_index(CIRC[1])
    for k in range(KC):
        target = jnp.broadcast_to(target_ref[:, k : k + 1], (1, LANES))
        targets_ref[k : k + 1, :] = target
        targets_ref[KC + k : KC + k + 1, :] = target - core
        targets_ref[2 * KC + k : 2 * KC + k + 1, :] = target - (1 - core)
    initial_ref[...] = tile_ref[pl.ds(pair % 4 * 2, 2), :]


def setup_body(b_hbm, c_hbm, bt_hbm, ct_ref, b_ref, c_ref, bt_ref, sems):
    part = b_ref.shape[0] // PARTS
    rows = [slice(k * part, (k + 1) * part) for k in range(PARTS)]
    weight = pltpu.make_async_copy(c_hbm, c_ref, sems.at[0])
    parts = [
        pltpu.make_async_copy(b_hbm.at[r], b_ref.at[r], sems.at[2 + k])
        for k, r in enumerate(rows)
    ]
    for copy in parts:
        copy.start()
    weight.start()
    for r, copy in zip(rows, parts):
        copy.wait()
        bt_ref[:, r] = b_ref[r, :].T
    turned = pltpu.make_async_copy(bt_ref, bt_hbm, sems.at[1])
    turned.start()
    weight.wait()
    ct_ref[...] = c_ref[...].T
    turned.wait()


def first_chain_body(terms_ref, initial_ref, start_ref):
    start = initial_ref[...]
    for n in range(64):
        start_ref[n] = start
        start = terms_ref[n, 2:4, :] * start + terms_ref[n, 0:2, :]


def chain_body(last_ref, terms_ref, old_ref, initial_ref, start_ref):
    start = initial_ref[...]
    for n in range(64):
        start_ref[n] = start
        decay = terms_ref[n, 2:4, :]
        start = decay * start + (last_ref[n] - decay * old_ref[n])


def group(target_ref, first, owner, blocks):
    total = None
    for k in range(KC):
        feeds = target_ref[first + k : first + k + 1, :] == owner
        term = jnp.where(feeds, blocks[:, k * PORTS : (k + 1) * PORTS], F32(0.0))
        total = term if total is None else total + term
    return total


def start_body(target_ref, pieces_ref, ct_ref, start_ref, out_ref):
    unpack(pieces_ref, start_ref)
    blocks = dot(start_ref[...].astype(BF16), ct_ref[...])
    for g in range(SUBS):
        out_ref[g] = group(target_ref, 0, g, blocks)


def free_body(start_ref, sources_ref, m_ref, bt_ref, ct_ref, z_ref, cz_ref, low_ref):
    previous = start_ref[...]
    for t in range(STEPS):
        drive = m_ref[...] * previous + sources_ref[t].astype(F32)
        previous = dot(drive.astype(BF16), bt_ref[...])
        z_ref[t * SCEN : (t + 1) * SCEN, :] = previous
        low_ref[t * SCEN : (t + 1) * SCEN, :] = previous.astype(BF16)
    cz_ref[...] = dot(low_ref[...], ct_ref[...])


def first_free_body(
    start_ref,
    sources_hbm,
    m_hbm,
    bt_hbm,
    ct_ref,
    z_ref,
    cz_ref,
    h_hbm,
    ch_ref,
    sources_ref,
    m_ref,
    bt_ref,
    h_ref,
    low_ref,
    both_ref,
    sems,
):
    part = bt_ref.shape[0] // PARTS
    rows = [slice(k * part, (k + 1) * part) for k in range(PARTS)]
    copies = [
        pltpu.make_async_copy(given, taken, sems.at[1 + k])
        for k, (given, taken) in enumerate(((m_hbm, m_ref), (sources_hbm, sources_ref)))
    ]
    parts = [
        pltpu.make_async_copy(bt_hbm.at[r], bt_ref.at[r], sems.at[3 + k])
        for k, r in enumerate(rows)
    ]
    for copy in copies + parts:
        copy.start()
    for copy in copies:
        copy.wait()
    previous = start_ref[...]
    for t in range(STEPS):
        drive = m_ref[...] * previous + sources_ref[t].astype(F32)
        if t == 0:
            drive = drive.astype(BF16)
            previous = jnp.zeros_like(previous)
            for r, copy in zip(rows, parts):
                copy.wait()
                previous = previous + dot(drive[:, r], bt_ref[r, :])
            response = bt_ref[0:PORTS, :]
            h_ref[0:PORTS, :] = response
            response = response.astype(F32)
        else:
            both_ref[0:SCEN, :] = drive.astype(BF16)
            both_ref[SCEN:, :] = (m_ref[...] * response).astype(BF16)
            both = dot(both_ref[...], bt_ref[...])
            previous, response = both[:SCEN], both[SCEN:]
            h_ref[t * PORTS : (t + 1) * PORTS, :] = response.astype(BF16)
        z_ref[t * SCEN : (t + 1) * SCEN, :] = previous
        low_ref[t * SCEN : (t + 1) * SCEN, :] = previous.astype(BF16)
    kept = pltpu.make_async_copy(h_ref, h_hbm, sems.at[0])
    kept.start()
    cz_ref[...] = dot(low_ref[...], ct_ref[...])
    ch_ref[...] = dot(h_ref[...], ct_ref[...]).astype(BF16)
    kept.wait()


def delays(inflow, x_ref):
    for k in range(STEPS):
        columns = slice(k * PORTS, (k + 1) * PORTS)
        if k:
            x_ref[0 : k * SCEN, columns] = jnp.zeros((k * SCEN, PORTS), BF16)
        x_ref[k * SCEN :, columns] = inflow[: (STEPS - k) * SCEN]


def couple_first_body(target_ref, f_ref, cz_ref, ch_ref, blocks_ref, out_ref, x_ref):
    inflow = jnp.sum(f_ref[...], axis=0).astype(BF16)
    delays(jnp.concatenate([inflow] * STEPS, axis=0), x_ref)
    blocks_ref[...] = cz_ref[...] + dot(x_ref[...], ch_ref[...])
    for g in range(CHIPS):
        out_ref[g] = group(target_ref, 2 * KC, 2 * g, blocks_ref[...])


def couple_body(target_ref, f_ref, cz_ref, ch_ref, blocks_ref, out_ref, x_ref):
    delays(jnp.sum(f_ref[...], axis=0).astype(BF16), x_ref)
    blocks_ref[...] = cz_ref[...] + dot(x_ref[...], ch_ref[...])
    for g in range(CHIPS):
        out_ref[g] = group(target_ref, 2 * KC, 2 * g, blocks_ref[...])


def gather_body(target_ref, blocks_ref, got_ref, out_ref):
    for g in range(CHIPS):
        out_ref[g] = got_ref[g] + group(target_ref, KC, 2 * g, blocks_ref[...])


def last_step_body(f_ref, z_ref, h_ref, out_ref, x_ref):
    inflow = jnp.sum(f_ref[...], axis=0).astype(BF16)
    for k in range(STEPS):
        t = STEPS - 1 - k
        x_ref[:, k * PORTS : (k + 1) * PORTS] = inflow[t * SCEN : (t + 1) * SCEN]
    pack(z_ref[(STEPS - 1) * SCEN :, :] + dot(x_ref[...], h_ref[...]), out_ref)


def wave_body(f_ref, z_ref, h_ref, out_ref, wave_ref, x_ref):
    delays(jnp.sum(f_ref[...], axis=0).astype(BF16), x_ref)
    wave = z_ref[...] + dot(x_ref[...], h_ref[...])
    wave_ref[...] = wave.astype(BF16)
    pack(wave[(STEPS - 1) * SCEN :, :], out_ref)


def finish_body(pieces_ref, wave_ref, state_ref, out_hbm, sem):
    copy = pltpu.make_async_copy(wave_ref, out_hbm, sem)
    copy.start()
    unpack(pieces_ref, state_ref)
    copy.wait()


def over_cuts(pieces):
    return lax.all_to_all(pieces, CUTS, 0, 0, tiled=True)


def over_circ(blocks):
    return lax.all_to_all(blocks, CIRC, 0, 0, tiled=True)


def over_chips(blocks):
    return lax.all_to_all(blocks, CIRC[0], 0, 0, tiled=True)


def other_core(blocks):
    return lax.ppermute(blocks, CIRC[1], [(0, 1), (1, 0)])


def shards(
    sources,
    block_inverse,
    memory_factor,
    coupling_target,
    coupling_weight,
    coarse_decay,
    initial_state,
):
    nodes = block_inverse.shape[-1]
    rows = STEPS * SCEN
    src = sources.reshape(STEPS, SCEN, nodes)
    inverse = block_inverse.reshape(nodes, nodes)
    weight = coupling_weight.reshape(KC * PORTS, nodes)
    factor = memory_factor.reshape(1, nodes)
    decay = coarse_decay.reshape(1, nodes)
    first = initial_state.reshape(SCEN, nodes)
    loads, targets, initial = call(
        load_body,
        [shape((64, 4, LANES)), shape((3 * KC, LANES), jnp.int32), shape((2, LANES))],
        (src, decay, coupling_target, first),
        "load",
        scratch=[
            pltpu.VMEM((STEPS, SCEN, nodes), BF16),
            pltpu.VMEM((1, nodes), F32),
            pltpu.VMEM((1, KC), jnp.int32),
            pltpu.VMEM((8, LANES), F32),
            pltpu.SemaphoreType.DMA((STEPS + 3,)),
        ],
        places=[HBM] * 4,
        grant=60,
    )
    terms = over_cuts(loads)
    bt, ct = call(
        setup_body,
        [shape((nodes, nodes), BF16), shape((nodes, KC * PORTS), BF16)],
        (inverse, weight),
        "setup",
        flops=2 * nodes * nodes * SCEN,
        scratch=[
            pltpu.VMEM((nodes, nodes), BF16),
            pltpu.VMEM((KC * PORTS, nodes), BF16),
            pltpu.VMEM((nodes, nodes), BF16),
            pltpu.SemaphoreType.DMA((2 + PARTS,)),
        ],
        places=[HBM] * 2,
        grant=52,
        out_places=[HBM, VMEM],
    )
    terms, bt, ct = lax.optimization_barrier((terms, bt, ct))
    (starts,) = call(first_chain_body, [shape((64, 2, LANES))], (terms, initial), "chain")
    pieces = over_cuts(starts)
    h = ch = wave = None
    for iteration in range(ITERS):
        start, sent = call(
            start_body,
            [shape((SCEN, nodes)), shape((SUBS, SCEN, PORTS))],
            (targets, pieces, ct),
            "start",
            flops=2 * SCEN * nodes * KC * PORTS,
        )
        inflow = over_circ(sent)
        given = (start, src, factor, bt, ct)
        free = [shape((rows, nodes)), shape((rows, KC * PORTS))]
        low = pltpu.VMEM((rows, nodes), BF16)
        flops = 2 * rows * nodes * (nodes + KC * PORTS)
        if iteration == 0:
            z, cz, h, ch = call(
                first_free_body,
                free
                + [shape((STEPS * PORTS, nodes), BF16), shape((STEPS * PORTS, KC * PORTS), BF16)],
                given,
                "free",
                flops=9 * flops,
                scratch=[
                    pltpu.VMEM((STEPS, SCEN, nodes), BF16),
                    pltpu.VMEM((1, nodes), F32),
                    pltpu.VMEM((nodes, nodes), BF16),
                    pltpu.VMEM((STEPS * PORTS, nodes), BF16),
                    low,
                    pltpu.VMEM((SCEN + PORTS, nodes), BF16),
                    pltpu.SemaphoreType.DMA((3 + PARTS,)),
                ],
                places=[VMEM, HBM, HBM, HBM, VMEM],
                grant=50,
                out_places=[VMEM, VMEM, HBM, VMEM],
            )
        else:
            z, cz = call(free_body, free, given, "free", flops=flops, scratch=[low])
        delayed = [pltpu.VMEM((rows, STEPS * PORTS), BF16)]
        for body in (couple_first_body, couple_body):
            blocks, sent = call(
                body,
                [shape((rows, KC * PORTS)), shape((CHIPS, rows, PORTS))],
                (targets, inflow, cz, ch),
                "couple",
                flops=2 * rows * nodes * KC * PORTS,
                scratch=delayed,
            )
            (sent,) = call(
                gather_body,
                [shape((CHIPS, rows, PORTS))],
                (targets, blocks, other_core(sent)),
                "gather",
            )
            inflow = over_chips(sent)
        if iteration < ITERS - 1:
            (last,) = call(
                last_step_body,
                [shape((64, 2, LANES))],
                (inflow, z, h),
                "last",
                flops=2 * SCEN * nodes * nodes,
                scratch=[pltpu.VMEM((SCEN, STEPS * PORTS), BF16)],
            )
        else:
            last, wave = call(
                wave_body,
                [shape((64, 2, LANES)), shape((rows, nodes), BF16)],
                (inflow, z, h),
                "wave",
                flops=2 * rows * nodes * nodes,
                scratch=delayed,
            )
        (starts,) = call(
            chain_body,
            [shape((64, 2, LANES))],
            (over_cuts(last), terms, starts, initial),
            "chain",
        )
        pieces = over_cuts(starts)
    start, wave = call(
        finish_body,
        [shape((SCEN, nodes)), shape((rows, nodes), BF16)],
        (pieces, wave),
        "finish",
        scratch=[pltpu.SemaphoreType.DMA],
        out_places=[VMEM, HBM],
    )
    return start.reshape(1, 1, SCEN, nodes), wave.reshape(1, STEPS, 1, SCEN, nodes)


def solution(mesh):
    finer = Mesh(mesh.devices.reshape(4, 2, 8, 4, 2), CUTS + CIRC)
    in_specs = (
        P(CUTS, None, CIRC, None, None),
        P(CIRC, None, None),
        P(CUTS, CIRC, None),
        P(CIRC, None),
        P(CIRC, None, None, None),
        P(CUTS, CIRC, None),
        P(CIRC, None, None),
    )
    out_specs = (P(CUTS, CIRC, None, None), P(CUTS, None, CIRC, None, None))
    return jax.shard_map(
        shards, mesh=finer, in_specs=in_specs, out_specs=out_specs, check_vma=False
    )
```

```python
import jax
import jax.numpy as jnp
from jax import lax
from jax.experimental import pallas as pl
from jax.experimental.pallas import tpu as pltpu
from jax.sharding import Mesh
from jax.sharding import PartitionSpec as P

ITERS = 2
STEPS = 8
SCEN = 16
PORTS = 128
KC = 4
SUBS = 8
CHIPS = 4
PARTS = 4
LANES = 128
CUTS = ("cuts_0", "cuts_1", "cuts_2")
CIRC = ("circ_0", "circ_1")
F32 = jnp.float32
BF16 = jnp.bfloat16
VMEM = pl.BlockSpec(memory_space=pltpu.VMEM)
HBM = pl.BlockSpec(memory_space=pl.ANY)


def shape(dims, dtype=F32):
    return jax.ShapeDtypeStruct(dims, dtype)


def call(body, outs, args, name, flops=0, scratch=(), places=None, grant=16, out_places=None):
    size = sum(a.size * a.dtype.itemsize for a in (*args, *outs))
    return pl.pallas_call(
        body,
        out_shape=outs,
        in_specs=places or [VMEM] * len(args),
        out_specs=out_places or [VMEM] * len(outs),
        scratch_shapes=list(scratch),
        compiler_params=pltpu.CompilerParams(vmem_limit_bytes=grant << 20),
        cost_estimate=pl.CostEstimate(flops=flops, bytes_accessed=size, transcendentals=0),
        name=name,
    )(*args)


def dot(a, b):
    return jnp.dot(a, b, preferred_element_type=F32)


def pack(state, out_ref, first=0):
    for b in range(state.shape[1] // LANES * 8):
        block, pair = divmod(b, 8)
        out_ref[first * 8 + b, 0:2, :] = state[
            2 * pair : 2 * pair + 2, block * LANES : (block + 1) * LANES
        ]


def unpack(pieces_ref, state_ref):
    for b in range(64):
        block, pair = divmod(b, 8)
        state_ref[2 * pair : 2 * pair + 2, block * LANES : (block + 1) * LANES] = pieces_ref[b]


def load_body(
    sources_ref,
    decay_ref,
    target_hbm,
    initial_hbm,
    out_hbm,
    targets_ref,
    initial_ref,
    held_ref,
    rate_ref,
    target_ref,
    tile_ref,
    out_ref,
    sems,
):
    block, pair = jnp.divmod(lax.axis_index(CUTS), 8)
    tile = initial_hbm.at[
        pl.ds(pl.multiple_of(pair // 4 * 8, 8), 8), pl.ds(pl.multiple_of(block * LANES, LANES), LANES)
    ]
    steps = [
        pltpu.make_async_copy(sources_ref.at[t], held_ref.at[t], sems.at[t]) for t in range(STEPS)
    ]
    small = [
        pltpu.make_async_copy(given, taken, sems.at[STEPS + k])
        for k, (given, taken) in enumerate(
            ((decay_ref, rate_ref), (target_hbm, target_ref), (tile, tile_ref))
        )
    ]
    for copy in small + steps:
        copy.start()
    for copy in small:
        copy.wait()
    for b in range(64):
        row = rate_ref[:, b // 8 * LANES : (b // 8 + 1) * LANES]
        out_ref[b, 2:4, :] = jnp.concatenate([row, row], axis=0)
    core = lax.axis_index(CIRC[1])
    for k in range(KC):
        target = jnp.broadcast_to(target_ref[:, k : k + 1], (1, LANES))
        targets_ref[k : k + 1, :] = target
        targets_ref[KC + k : KC + k + 1, :] = target - core
        targets_ref[2 * KC + k : 2 * KC + k + 1, :] = target - (1 - core)
    initial_ref[...] = tile_ref[pl.ds(pair % 4 * 2, 2), :]
    for copy in steps:
        copy.wait()
    sent = []
    for k in range(8):
        columns = slice(k * LANES, (k + 1) * LANES)
        total = held_ref[0, :, columns].astype(F32)
        for t in range(1, STEPS):
            total = total + held_ref[t, :, columns].astype(F32)
        pack(total * (1.0 / STEPS), out_ref, k)
        pieces = slice(8 * k, 8 * k + 8)
        sent.append(
            pltpu.make_async_copy(
                out_ref.at[pieces], out_hbm.at[pieces], sems.at[STEPS + 3 + k]
            )
        )
        sent[-1].start()
    for copy in sent:
        copy.wait()


def setup_body(b_hbm, c_hbm, bt_hbm, ct_ref, b_ref, c_ref, bt_ref, sems):
    part = b_ref.shape[0] // PARTS
    rows = [slice(k * part, (k + 1) * part) for k in range(PARTS)]
    weight = pltpu.make_async_copy(c_hbm, c_ref, sems.at[0])
    parts = [
        pltpu.make_async_copy(b_hbm.at[r], b_ref.at[r], sems.at[2 + k])
        for k, r in enumerate(rows)
    ]
    for copy in parts:
        copy.start()
    weight.start()
    for r, copy in zip(rows, parts):
        copy.wait()
        bt_ref[:, r] = b_ref[r, :].T
    turned = pltpu.make_async_copy(bt_ref, bt_hbm, sems.at[1])
    turned.start()
    weight.wait()
    ct_ref[...] = c_ref[...].T
    turned.wait()


def first_chain_body(terms_ref, initial_ref, start_ref):
    start = initial_ref[...]
    for n in range(64):
        start_ref[n] = start
        start = terms_ref[n, 2:4, :] * start + terms_ref[n, 0:2, :]


def chain_body(last_ref, terms_ref, old_ref, initial_ref, start_ref):
    start = initial_ref[...]
    for n in range(64):
        start_ref[n] = start
        decay = terms_ref[n, 2:4, :]
        start = decay * start + (last_ref[n] - decay * old_ref[n])


def group(target_ref, first, owner, blocks):
    total = None
    for k in range(KC):
        feeds = target_ref[first + k : first + k + 1, :] == owner
        term = jnp.where(feeds, blocks[:, k * PORTS : (k + 1) * PORTS], F32(0.0))
        total = term if total is None else total + term
    return total


def start_body(target_ref, pieces_ref, ct_ref, start_ref, out_ref):
    unpack(pieces_ref, start_ref)
    blocks = dot(start_ref[...].astype(BF16), ct_ref[...])
    for g in range(SUBS):
        out_ref[g] = group(target_ref, 0, g, blocks)


def free_body(start_ref, sources_ref, m_ref, bt_ref, ct_ref, z_ref, cz_ref, low_ref):
    previous = start_ref[...]
    for t in range(STEPS):
        drive = m_ref[...] * previous + sources_ref[t].astype(F32)
        previous = dot(drive.astype(BF16), bt_ref[...])
        z_ref[t * SCEN : (t + 1) * SCEN, :] = previous
        low_ref[t * SCEN : (t + 1) * SCEN, :] = previous.astype(BF16)
    cz_ref[...] = dot(low_ref[...], ct_ref[...])


def first_free_body(
    start_ref,
    sources_hbm,
    m_hbm,
    bt_hbm,
    ct_ref,
    z_ref,
    cz_ref,
    h_hbm,
    ch_ref,
    sources_ref,
    m_ref,
    bt_ref,
    h_ref,
    low_ref,
    both_ref,
    sems,
):
    part = bt_ref.shape[0] // PARTS
    rows = [slice(k * part, (k + 1) * part) for k in range(PARTS)]
    copies = [
        pltpu.make_async_copy(given, taken, sems.at[1 + k])
        for k, (given, taken) in enumerate(((m_hbm, m_ref), (sources_hbm, sources_ref)))
    ]
    parts = [
        pltpu.make_async_copy(bt_hbm.at[r], bt_ref.at[r], sems.at[3 + k])
        for k, r in enumerate(rows)
    ]
    for copy in copies + parts:
        copy.start()
    for copy in copies:
        copy.wait()
    previous = start_ref[...]
    for t in range(STEPS):
        drive = m_ref[...] * previous + sources_ref[t].astype(F32)
        if t == 0:
            drive = drive.astype(BF16)
            previous = jnp.zeros_like(previous)
            for r, copy in zip(rows, parts):
                copy.wait()
                previous = previous + dot(drive[:, r], bt_ref[r, :])
            response = bt_ref[0:PORTS, :]
            h_ref[0:PORTS, :] = response
            response = response.astype(F32)
        else:
            both_ref[0:SCEN, :] = drive.astype(BF16)
            both_ref[SCEN:, :] = (m_ref[...] * response).astype(BF16)
            both = dot(both_ref[...], bt_ref[...])
            previous, response = both[:SCEN], both[SCEN:]
            h_ref[t * PORTS : (t + 1) * PORTS, :] = response.astype(BF16)
        z_ref[t * SCEN : (t + 1) * SCEN, :] = previous
        low_ref[t * SCEN : (t + 1) * SCEN, :] = previous.astype(BF16)
    kept = pltpu.make_async_copy(h_ref, h_hbm, sems.at[0])
    kept.start()
    cz_ref[...] = dot(low_ref[...], ct_ref[...])
    ch_ref[...] = dot(h_ref[...], ct_ref[...]).astype(BF16)
    kept.wait()


def delays(inflow, x_ref):
    for k in range(STEPS):
        columns = slice(k * PORTS, (k + 1) * PORTS)
        if k:
            x_ref[0 : k * SCEN, columns] = jnp.zeros((k * SCEN, PORTS), BF16)
        x_ref[k * SCEN :, columns] = inflow[: (STEPS - k) * SCEN]


def couple_first_body(target_ref, f_ref, cz_ref, ch_ref, blocks_ref, out_ref, x_ref):
    inflow = jnp.sum(f_ref[...], axis=0).astype(BF16)
    delays(jnp.concatenate([inflow] * STEPS, axis=0), x_ref)
    blocks_ref[...] = cz_ref[...] + dot(x_ref[...], ch_ref[...])
    for g in range(CHIPS):
        out_ref[g] = group(target_ref, 2 * KC, 2 * g, blocks_ref[...])


def couple_body(target_ref, f_ref, cz_ref, ch_ref, blocks_ref, out_ref, x_ref):
    delays(jnp.sum(f_ref[...], axis=0).astype(BF16), x_ref)
    blocks_ref[...] = cz_ref[...] + dot(x_ref[...], ch_ref[...])
    for g in range(CHIPS):
        out_ref[g] = group(target_ref, 2 * KC, 2 * g, blocks_ref[...])


def gather_body(target_ref, blocks_ref, got_ref, out_ref):
    for g in range(CHIPS):
        out_ref[g] = got_ref[g] + group(target_ref, KC, 2 * g, blocks_ref[...])


def last_step_body(f_ref, z_ref, h_ref, out_ref, x_ref):
    inflow = jnp.sum(f_ref[...], axis=0).astype(BF16)
    for k in range(STEPS):
        t = STEPS - 1 - k
        x_ref[:, k * PORTS : (k + 1) * PORTS] = inflow[t * SCEN : (t + 1) * SCEN]
    pack(z_ref[(STEPS - 1) * SCEN :, :] + dot(x_ref[...], h_ref[...]), out_ref)


def wave_body(f_ref, z_ref, h_ref, out_ref, wave_ref, x_ref):
    delays(jnp.sum(f_ref[...], axis=0).astype(BF16), x_ref)
    wave = z_ref[...] + dot(x_ref[...], h_ref[...])
    wave_ref[...] = wave.astype(BF16)
    pack(wave[(STEPS - 1) * SCEN :, :], out_ref)


def finish_body(pieces_ref, wave_ref, state_ref, out_hbm, sem):
    copy = pltpu.make_async_copy(wave_ref, out_hbm, sem)
    copy.start()
    unpack(pieces_ref, state_ref)
    copy.wait()


def over_cuts(pieces):
    return lax.all_to_all(pieces, CUTS, 0, 0, tiled=True)


def over_circ(blocks):
    return lax.all_to_all(blocks, CIRC, 0, 0, tiled=True)


def over_chips(blocks):
    return lax.all_to_all(blocks, CIRC[0], 0, 0, tiled=True)


def other_core(blocks):
    return lax.ppermute(blocks, CIRC[1], [(0, 1), (1, 0)])


def shards(
    sources,
    block_inverse,
    memory_factor,
    coupling_target,
    coupling_weight,
    coarse_decay,
    initial_state,
):
    nodes = block_inverse.shape[-1]
    rows = STEPS * SCEN
    src = sources.reshape(STEPS, SCEN, nodes)
    inverse = block_inverse.reshape(nodes, nodes)
    weight = coupling_weight.reshape(KC * PORTS, nodes)
    factor = memory_factor.reshape(1, nodes)
    decay = coarse_decay.reshape(1, nodes)
    first = initial_state.reshape(SCEN, nodes)
    loads, targets, initial = call(
        load_body,
        [shape((64, 4, LANES)), shape((3 * KC, LANES), jnp.int32), shape((2, LANES))],
        (src, decay, coupling_target, first),
        "load",
        scratch=[
            pltpu.VMEM((STEPS, SCEN, nodes), BF16),
            pltpu.VMEM((1, nodes), F32),
            pltpu.VMEM((1, KC), jnp.int32),
            pltpu.VMEM((8, LANES), F32),
            pltpu.VMEM((64, 4, LANES), F32),
            pltpu.SemaphoreType.DMA((STEPS + 11,)),
        ],
        places=[HBM] * 4,
        grant=60,
        out_places=[HBM, VMEM, VMEM],
    )
    terms = over_cuts(loads)
    bt, ct = call(
        setup_body,
        [shape((nodes, nodes), BF16), shape((nodes, KC * PORTS), BF16)],
        (inverse, weight),
        "setup",
        flops=2 * nodes * nodes * SCEN,
        scratch=[
            pltpu.VMEM((nodes, nodes), BF16),
            pltpu.VMEM((KC * PORTS, nodes), BF16),
            pltpu.VMEM((nodes, nodes), BF16),
            pltpu.SemaphoreType.DMA((2 + PARTS,)),
        ],
        places=[HBM] * 2,
        grant=52,
        out_places=[HBM, VMEM],
    )
    terms, bt, ct = lax.optimization_barrier((terms, bt, ct))
    (starts,) = call(first_chain_body, [shape((64, 2, LANES))], (terms, initial), "chain")
    pieces = over_cuts(starts)
    h = ch = wave = None
    for iteration in range(ITERS):
        start, sent = call(
            start_body,
            [shape((SCEN, nodes)), shape((SUBS, SCEN, PORTS))],
            (targets, pieces, ct),
            "start",
            flops=2 * SCEN * nodes * KC * PORTS,
        )
        inflow = over_circ(sent)
        given = (start, src, factor, bt, ct)
        free = [shape((rows, nodes)), shape((rows, KC * PORTS))]
        low = pltpu.VMEM((rows, nodes), BF16)
        flops = 2 * rows * nodes * (nodes + KC * PORTS)
        if iteration == 0:
            z, cz, h, ch = call(
                first_free_body,
                free
                + [shape((STEPS * PORTS, nodes), BF16), shape((STEPS * PORTS, KC * PORTS), BF16)],
                given,
                "free",
                flops=9 * flops,
                scratch=[
                    pltpu.VMEM((STEPS, SCEN, nodes), BF16),
                    pltpu.VMEM((1, nodes), F32),
                    pltpu.VMEM((nodes, nodes), BF16),
                    pltpu.VMEM((STEPS * PORTS, nodes), BF16),
                    low,
                    pltpu.VMEM((SCEN + PORTS, nodes), BF16),
                    pltpu.SemaphoreType.DMA((3 + PARTS,)),
                ],
                places=[VMEM, HBM, HBM, HBM, VMEM],
                grant=50,
                out_places=[VMEM, VMEM, HBM, VMEM],
            )
        else:
            z, cz = call(free_body, free, given, "free", flops=flops, scratch=[low])
        delayed = [pltpu.VMEM((rows, STEPS * PORTS), BF16)]
        for body in (couple_first_body, couple_body):
            blocks, sent = call(
                body,
                [shape((rows, KC * PORTS)), shape((CHIPS, rows, PORTS))],
                (targets, inflow, cz, ch),
                "couple",
                flops=2 * rows * nodes * KC * PORTS,
                scratch=delayed,
            )
            (sent,) = call(
                gather_body,
                [shape((CHIPS, rows, PORTS))],
                (targets, blocks, other_core(sent)),
                "gather",
            )
            inflow = over_chips(sent)
        if iteration < ITERS - 1:
            (last,) = call(
                last_step_body,
                [shape((64, 2, LANES))],
                (inflow, z, h),
                "last",
                flops=2 * SCEN * nodes * nodes,
                scratch=[pltpu.VMEM((SCEN, STEPS * PORTS), BF16)],
            )
        else:
            last, wave = call(
                wave_body,
                [shape((64, 2, LANES)), shape((rows, nodes), BF16)],
                (inflow, z, h),
                "wave",
                flops=2 * rows * nodes * nodes,
                scratch=delayed,
            )
        (starts,) = call(
            chain_body,
            [shape((64, 2, LANES))],
            (over_cuts(last), terms, starts, initial),
            "chain",
        )
        pieces = over_cuts(starts)
    start, wave = call(
        finish_body,
        [shape((SCEN, nodes)), shape((rows, nodes), BF16)],
        (pieces, wave),
        "finish",
        scratch=[pltpu.SemaphoreType.DMA],
        out_places=[VMEM, HBM],
    )
    return start.reshape(1, 1, SCEN, nodes), wave.reshape(1, STEPS, 1, SCEN, nodes)


def solution(mesh):
    finer = Mesh(mesh.devices.reshape(4, 2, 8, 4, 2), CUTS + CIRC)
    in_specs = (
        P(CUTS, None, CIRC, None, None),
        P(CIRC, None, None),
        P(CUTS, CIRC, None),
        P(CIRC, None),
        P(CIRC, None, None, None),
        P(CUTS, CIRC, None),
        P(CIRC, None, None),
    )
    out_specs = (P(CUTS, CIRC, None, None), P(CUTS, None, CIRC, None, None))
    return jax.shard_map(
        shards, mesh=finer, in_specs=in_specs, out_specs=out_specs, check_vma=False
    )
```
